32 devices in a mesh: ctx: 8 (over z, y), tp: 4 (over x, core).
Axes of the slice: x: 2, y: 2, z: 4, core: 2. Of those that a mesh axis runs over, the one named last changes fastest.
Arguments:
- queries: bfloat16 [32, 128, 128], P('ctx', 'tp'), may hold values from -60 to 60
- cached_keys: bfloat16 [16384, 8, 128], P('ctx', 'tp'), may hold values from -6 to 6
- cached_values: bfloat16 [16384, 8, 128], P('ctx', 'tp'), may hold values from -6 to 6
- cached_pos: int32 [16384], P('ctx'), may hold values from -1 to 16383, as said below
- new_keys: bfloat16 [32, 8, 128], P('ctx', 'tp'), may hold values from -9 to 9
- new_values: bfloat16 [32, 8, 128], P('ctx', 'tp'), may hold values from -6 to 6
- new_pos: int32 [32], replicated, may hold values from 16384 to 16415, as said below
- out_weight: bfloat16 [16384, 16384], P('tp', 'ctx'), may hold values from -0.046875 to 0.046875
Outputs:
- context: bfloat16 [32, 16384], P('ctx', 'tp')
- projected: bfloat16 [32, 16384], P('tp', 'ctx')
The draws below stay inside these ranges and needn't reach their ends.
Inputs may be any that keep to these rules, and one draw needn't show every extreme that they name: `cached_pos`: each index of ctx holds 2048 slots; the filled ones come first in its block, at least a quarter of them; some block is full; filled slots carry distinct positions below 16384. `new_pos`: distinct positions following the cache.
All inputs are finite; a program needn't handle non-finite values.
Results may differ from the reference program's by a relative error of at most 0.015.
Values may be sent and summed in bfloat16 or wider, within the bound.
A program may use at most 128 MiB of HBM per device.

```python
import math
import jax
import jax.numpy as jnp
from jax import lax

D = 16384
HQ = 128
KVH = 8
DH = 128
CACHE_DEV = 2048
GROUP = 16
CACHE = 16384
NEW = 32


def shared_keys(key):
    return jnp.clip(jax.random.normal(key, (CACHE, KVH, DH), jnp.float32), -6.0, 6.0)


def draw_cached_keys(key, part):
    base = shared_keys(key)
    return base.astype(jnp.bfloat16)


def draw_queries(key, part):
    key = jax.random.fold_in(key, 2)
    result = jnp.clip(3.0 * jax.random.normal(key, (NEW, HQ, DH), jnp.float32), -24.0, 24.0)
    return result.astype(jnp.bfloat16)


def draw_cached_pos(key, part):
    key = jax.random.fold_in(key, 3)
    key_a, key_b, key_c = jax.random.split(key, 3)
    nblk = CACHE // CACHE_DEV
    shifts = jax.random.randint(key_a, (nblk,), 0, 3)
    full_block = jax.random.randint(key_b, (), 0, nblk)
    counts = jnp.right_shift(jnp.full((nblk,), CACHE_DEV, jnp.int32), shifts.astype(jnp.int32))
    counts = jnp.where(jnp.arange(nblk) == full_block, CACHE_DEV, counts)
    slots = jnp.arange(CACHE)
    filled = slots % CACHE_DEV < counts[slots // CACHE_DEV]
    order = jax.random.permutation(key_c, CACHE).astype(jnp.int32)
    target = (full_block * CACHE_DEV).astype(jnp.int32)
    holder = jnp.argmax(order == CACHE - 1).astype(jnp.int32)
    displaced = order[target]
    order = order.at[holder].set(displaced)
    order = order.at[target].set(CACHE - 1)
    return jnp.where(filled, order, -1).astype(jnp.int32)


def draw_new_pos(key, part):
    key = jax.random.fold_in(key, 4)
    return (CACHE + jax.random.permutation(key, NEW)).astype(jnp.int32)


def level_of(own_key, shape, cuts, least, high):
    gain, own = 1.0, jax.random.fold_in(own_key, 6)
    for dim, parts in cuts:
        steps = jnp.exp(jax.random.uniform(jax.random.fold_in(own, dim), (parts,), jnp.float32, least / len(cuts), high / len(cuts)))
        gain = gain * jnp.repeat(steps, shape[dim] // parts).reshape([-1 if axis == dim else 1 for axis in range(len(shape))])
    return gain


def gaussian(stream_key, shape, width, limit, pieces=(), dtype=jnp.bfloat16):
    values = jax.random.normal(stream_key, shape, jnp.float32) * width
    if len(pieces) > 0:
        values = level_of(stream_key, shape, pieces, -0.22, 0.18) * values
    return jnp.clip(values, min=-limit, max=limit).astype(dtype)


def setup_inputs(seed: int = 0) -> dict:
    streams_of = jax.random.split(jax.random.key(seed), 9)
    queries = draw_queries(jax.random.fold_in(streams_of[8], 71), 0)
    cached_keys = draw_cached_keys(jax.random.fold_in(streams_of[8], 71), 0)
    cached_values = gaussian(streams_of[2], (CACHE, KVH, DH), 1.0, 6.0, ((0, 8), (1, 4)))
    cached_pos = draw_cached_pos(jax.random.fold_in(streams_of[8], 71), 0)
    new_keys = gaussian(streams_of[4], (NEW, KVH, DH), 1.6, 9.0, ((0, 8), (1, 4)))
    new_values = gaussian(streams_of[5], (NEW, KVH, DH), 1.0, 6.0, ((0, 8), (1, 4)))
    new_pos = draw_new_pos(jax.random.fold_in(streams_of[8], 71), 0)
    out_weight = gaussian(streams_of[7], (HQ * DH, D), (HQ * DH) ** -0.5, 0.046875, ((0, 4), (1, 8)))
    return {"queries": queries, "cached_keys": cached_keys, "cached_values": cached_values, "cached_pos": cached_pos, "new_keys": new_keys, "new_values": new_values, "new_pos": new_pos, "out_weight": out_weight}


masked_score = -1e+30

def tile(q4, keys, values, qpos, kpos, scale):
    s = jnp.einsum('rhgd,khd->rhgk', q4.astype(jnp.float32), keys.astype(jnp.float32), precision=lax.Precision.HIGHEST) * scale
    allow = ((kpos[None, :] >= 0) & (kpos[None, :] <= qpos[:, None]))[:, None, None, :]
    s = jnp.where(allow, s, masked_score)
    top = lax.optimization_barrier(jnp.max(s, axis=-1))
    weights = jnp.where(allow, jnp.exp(s - top[..., None]), 0.0)
    total = lax.optimization_barrier(jnp.sum(weights, axis=-1))
    rounded = lax.optimization_barrier(weights.astype(jnp.bfloat16)).astype(jnp.float32)
    numer = jnp.einsum('rhgk,khd->rhgd', rounded, values.astype(jnp.float32), precision=lax.Precision.HIGHEST)
    return (numer, top, total)

def combine_parts(first, second):
    top = jnp.maximum(first[1], second[1])
    factor_a = jnp.exp(first[1] - top)
    factor_b = jnp.exp(second[1] - top)
    numer = first[0] * factor_a[..., None] + second[0] * factor_b[..., None]
    return (numer, top, first[2] * factor_a + second[2] * factor_b)

def reference(queries, cached_keys, cached_values, cached_pos, new_keys, new_values, new_pos, out_weight):
    scale = 1.0 / math.sqrt(DH)
    q4 = queries.reshape(NEW, KVH, GROUP, DH)
    block = math.gcd(CACHE_DEV, 512)
    nblk = CACHE // block
    key_blocks = cached_keys.reshape(nblk, block, KVH, DH)
    value_blocks = cached_values.reshape(nblk, block, KVH, DH)
    pos_blocks = cached_pos.reshape(nblk, block)
    start = (jnp.zeros((NEW, KVH, GROUP, DH), jnp.float32), jnp.full((NEW, KVH, GROUP), masked_score, jnp.float32), jnp.zeros((NEW, KVH, GROUP), jnp.float32))

    def step(carry, blk):
        return (combine_parts(carry, tile(q4, blk[0], blk[1], new_pos, blk[2], scale)), None)
    carry, _ = lax.scan(step, start, (key_blocks, value_blocks, pos_blocks))
    carry = combine_parts(carry, tile(q4, new_keys, new_values, new_pos, new_pos, scale))
    context = (carry[0] / carry[2][..., None]).astype(jnp.bfloat16).reshape(NEW, HQ * DH)
    projected = jnp.dot(context, out_weight, preferred_element_type=jnp.float32).astype(jnp.bfloat16)
    return (context, projected)
```

```python
import functools
import math

import jax
import jax.numpy as jnp
from jax import lax
from jax.experimental import pallas as pl
from jax.experimental.pallas import tpu as pltpu
from jax.sharding import PartitionSpec as P

masked_score = -1e30
MESH = pl.DeviceIdType.MESH
lanes = 128
new_pad = 128
col_tiles = 4
bf16 = jnp.bfloat16
f32 = jnp.float32


def kernel(
    n, ntp, local_new, kv_heads, group, slots,
    q_ref, k_hbm, v_hbm, pos_ref, nk_ref, nv_ref, newpos_ref, w_hbm,
    ctx_out, proj_out,
    kraw, vraw, kh, vh, wide, small, bias_c, bias_n, qall, wbuf,
    onum, rnum, sstat, rstat, wts, cown, call, cf, lhs, acc, dsend, drecv,
    k_sem, v_sem, w_sem, q_send, q_recv, n_send, n_recv, s_send, s_recv,
    c_send, c_recv, d_send, d_recv,
):
    me = lax.axis_index("ctx")
    tp = lax.axis_index("tp")
    rows = local_new * group
    per_chunk = lanes // rows
    chunks = n // per_chunk
    mine = me // per_chunk
    tokens = n * local_new
    depth = group * lanes
    coef = math.log2(math.e) / math.sqrt(lanes)

    k_copy = pltpu.make_async_copy(k_hbm, kraw, k_sem)
    v_copy = pltpu.make_async_copy(v_hbm, vraw, v_sem)
    k_copy.start()
    v_copy.start()
    w_parts = 4 * kv_heads
    w_rows = kv_heads * depth // w_parts
    w_copies = [
        pltpu.make_async_copy(
            w_hbm.at[pl.ds(i * w_rows, w_rows)], wbuf.at[pl.ds(i * w_rows, w_rows)], w_sem.at[i]
        )
        for i in range(w_parts)
    ]
    for copy in w_copies:
        copy.start()

    barrier = pltpu.get_barrier_semaphore()

    def greet(i, _):
        pl.semaphore_signal(
            barrier, inc=1, device_id={"ctx": lax.rem(me + i, n)}, device_id_type=MESH
        )
        return 0

    lax.fori_loop(1, n, greet, 0)
    for i in range(1, ntp):
        pl.semaphore_signal(
            barrier, inc=1, device_id={"tp": lax.rem(tp + i, ntp)}, device_id_type=MESH
        )
    pl.semaphore_wait(barrier, n - 1 + ntp - 1)

    def q_copy(slot, peer):
        return pltpu.make_async_remote_copy(
            src_ref=q_ref,
            dst_ref=qall.at[pl.ds(slot * local_new, local_new)],
            send_sem=q_send.at[peer],
            recv_sem=q_recv.at[slot],
            device_id={"ctx": peer},
            device_id_type=MESH,
        )

    def num_copy(h, peer, slot):
        return pltpu.make_async_remote_copy(
            src_ref=onum.at[h, peer],
            dst_ref=rnum.at[h, slot],
            send_sem=n_send.at[h, peer],
            recv_sem=n_recv.at[h, slot],
            device_id={"ctx": peer},
            device_id_type=MESH,
        )

    def stat_copy(h, peer, slot):
        return pltpu.make_async_remote_copy(
            src_ref=sstat.at[h, peer // per_chunk],
            dst_ref=rstat.at[pl.ds((h * n + slot) * 8, 8)],
            send_sem=s_send.at[h, peer],
            recv_sem=s_recv.at[h, slot],
            device_id={"ctx": peer},
            device_id_type=MESH,
        )

    def ctx_copy(h, peer, slot):
        return pltpu.make_async_remote_copy(
            src_ref=call.at[h, slot],
            dst_ref=call.at[h, slot],
            send_sem=c_send.at[h, peer],
            recv_sem=c_recv.at[h, slot],
            device_id={"ctx": peer},
            device_id_type=MESH,
        )

    def part_copy(j, peer, slot):
        return pltpu.make_async_remote_copy(
            src_ref=dsend.at[j, peer],
            dst_ref=drecv.at[j, slot],
            send_sem=d_send.at[j, peer],
            recv_sem=d_recv.at[j, slot],
            device_id={"tp": peer},
            device_id_type=MESH,
        )

    def others(body):
        def step(i, _):
            body(lax.rem(me + i, n))
            return 0

        lax.fori_loop(1, n, step, 0)

    def send_queries(i, _):
        c = lax.rem(mine + chunks - i, chunks)
        for j in range(per_chunk):
            peer = c * per_chunk + j

            @pl.when(peer != me)
            def _():
                q_copy(me, peer).start()

        return 0

    lax.fori_loop(0, chunks, send_queries, 0)
    qall[pl.ds(me * local_new, local_new)] = q_ref[...]

    bias_c[...] = jnp.where(pos_ref[...] >= 0, 0.0, masked_score)
    lane = lax.broadcasted_iota(jnp.int32, (group, lanes), 1)
    key_pos = jnp.full((group, lanes), 2**30, jnp.int32)
    for j in range(local_new):
        key_pos = jnp.where(lane == j, newpos_ref[me * local_new + j], key_pos)

    def mask_new(t, _):
        bias_n[pl.ds(t * group, group), :] = jnp.where(
            key_pos <= newpos_ref[t], 0.0, masked_score
        )
        return 0

    lax.fori_loop(0, tokens, mask_new, 0)

    part = math.gcd(slots, 256)

    def split_heads(raw, new_ref, out):
        def step(i, _):
            wide[...] = raw[pl.ds(i * part * kv_heads, part * kv_heads), :].astype(f32)
            for h in range(kv_heads):
                out[h, pl.ds(i * part, part), :] = wide[
                    pl.ds(h, part, stride=kv_heads), :
                ].astype(bf16)
            return 0

        lax.fori_loop(0, slots // part, step, 0)
        wide[pl.ds(0, local_new * kv_heads), :] = new_ref[...].astype(f32)
        for h in range(kv_heads):
            small[...] = jnp.zeros_like(small)
            small[pl.ds(0, local_new), :] = wide[pl.ds(h, local_new, stride=kv_heads), :]
            out[h, pl.ds(slots, new_pad), :] = small[...].astype(bf16)

    k_copy.wait()
    split_heads(kraw, nk_ref, kh)
    v_copy.wait()
    split_heads(vraw, nv_ref, vh)

    diag = lax.broadcasted_iota(jnp.int32, (lanes, lanes), 0) == lax.broadcasted_iota(
        jnp.int32, (lanes, lanes), 1
    )

    def attend(h):
        def step(i, _):
            c = lax.rem(mine + i, chunks)
            if h == 0:
                for j in range(per_chunk):
                    peer = c * per_chunk + j

                    @pl.when(peer != me)
                    def _():
                        q_copy(peer, peer).wait_recv()

            tok = c * per_chunk * local_new
            q = qall[pl.ds(tok, per_chunk * local_new), pl.ds(h * group, group), :]
            q = q.reshape(lanes, lanes)
            s = lax.dot_general(
                q, kh[h], (((1,), (1,)), ((), ())), preferred_element_type=f32
            )
            old = s[:, :slots] + bias_c[...]
            new = s[:, slots:] + bias_n[pl.ds(tok * group, lanes), :]
            top = jnp.maximum(
                jnp.max(old, axis=1, keepdims=True), jnp.max(new, axis=1, keepdims=True)
            )
            old = jnp.exp2((old - top) * coef)
            new = jnp.exp2((new - top) * coef)
            total = jnp.sum(old, axis=1, keepdims=True) + jnp.sum(new, axis=1, keepdims=True)
            out = jnp.dot(old.astype(bf16), vh[h, :slots], preferred_element_type=f32)
            out += jnp.dot(new.astype(bf16), vh[h, slots:], preferred_element_type=f32)
            out = (out / total).astype(bf16)
            level = top * coef + jnp.log2(total)
            stat = jnp.sum(jnp.where(diag, level, 0.0), axis=0, keepdims=True)
            stat = jnp.broadcast_to(stat, (8, lanes))
            sstat[h, c] = stat
            for j in range(per_chunk):
                peer = c * per_chunk + j
                onum[h, peer] = out[j * rows : (j + 1) * rows]

                @pl.when(peer != me)
                def _():
                    stat_copy(h, peer, me).start()
                    num_copy(h, peer, me).start()

                @pl.when(peer == me)
                def _():
                    rnum[h, me] = out[j * rows : (j + 1) * rows]
                    rstat[pl.ds((h * n + me) * 8, 8), :] = stat

            return 0

        lax.fori_loop(0, chunks, step, 0)

    def combine(h):
        def arrived(peer):
            stat_copy(h, peer, peer).wait_recv()
            num_copy(h, peer, peer).wait_recv()

        others(arrived)
        level = rstat[pl.ds(h * n * 8, n, stride=8), :]
        factor = jnp.exp2(level - jnp.max(level, axis=0, keepdims=True))
        factor = factor / jnp.sum(factor, axis=0, keepdims=True)
        wts[...] = factor.T
        first = pl.multiple_of(lax.rem(me, per_chunk) * rows, rows)
        weight = wts[pl.ds(first, rows), :]
        context = jnp.zeros((rows, lanes), f32)
        for s in range(n):
            context += rnum[h, s].astype(f32) * weight[:, s : s + 1]
        call[h, me] = context.astype(bf16)
        others(lambda peer: ctx_copy(h, peer, me).start())
        cown[...] = context
        for g in range(group):
            at = (h * group + g) * lanes
            ctx_out[:, at : at + lanes] = cown[pl.ds(g, local_new, stride=group), :].astype(bf16)

    tile = proj_out.shape[1] // col_tiles
    half = tile // 2
    block = tokens // ntp

    def project(h):
        others(lambda peer: ctx_copy(h, peer, peer).wait_recv())
        cf[...] = call[h].reshape(tokens * group, lanes).astype(f32)
        for g in range(group):
            lhs[:, g * lanes : (g + 1) * lanes] = cf[pl.ds(g, tokens, stride=group), :].astype(bf16)
        for copy in w_copies[h * 4 : (h + 1) * 4]:
            copy.wait()
        for j in range(col_tiles):
            cols = slice(j * tile, (j + 1) * tile)
            term = jnp.dot(
                lhs[...], wbuf[h * depth : (h + 1) * depth, cols], preferred_element_type=f32
            )
            if h > 0:
                term += acc[:, cols]
            if h < kv_heads - 1:
                acc[:, cols] = term
                continue
            for r in range(ntp):
                slab = term[r * block : (r + 1) * block]
                slab = jnp.concatenate([slab[:, :half], slab[:, half:]], axis=0).astype(bf16)
                dsend[j, r] = slab

                @pl.when(tp != r)
                def _():
                    part_copy(j, r, tp).start()

                @pl.when(tp == r)
                def _():
                    drecv[j, tp] = slab

    for h in range(kv_heads):
        attend(h)
    for h in range(kv_heads):
        combine(h)
    for h in range(kv_heads):
        project(h)

    for j in range(col_tiles):
        for i in range(1, ntp):
            peer = lax.rem(tp + i, ntp)
            part_copy(j, peer, peer).wait_recv()
        total = drecv[j, 0].astype(f32)
        for r in range(1, ntp):
            total += drecv[j, r].astype(f32)
        proj_out[:, j * tile : (j + 1) * tile] = jnp.concatenate(
            [total[:block], total[block:]], axis=1
        ).astype(bf16)

    def sent(peer):
        q_copy(me, peer).wait_send()
        for h in range(kv_heads):
            num_copy(h, peer, me).wait_send()
            stat_copy(h, peer, me).wait_send()
            ctx_copy(h, peer, me).wait_send()

    others(sent)
    for j in range(col_tiles):
        for i in range(1, ntp):
            part_copy(j, lax.rem(tp + i, ntp), tp).wait_send()


def per_device(
    n, ntp, queries, cached_keys, cached_values, cached_pos, new_keys, new_values, new_pos,
    out_weight,
):
    local_new, heads, head_size = queries.shape
    slots, kv_heads = cached_keys.shape[:2]
    group = heads // kv_heads
    rows = local_new * group
    tokens = n * local_new
    depth, cols = out_weight.shape
    chunks = n // (lanes // rows)
    all_keys = slots + new_pad
    block = tokens // ntp
    half = cols // col_tiles // 2
    vmem = pl.BlockSpec(memory_space=pltpu.VMEM)
    hbm = pl.BlockSpec(memory_space=pl.ANY)
    dma = pltpu.SemaphoreType.DMA
    flops = 4 * tokens * heads * slots * head_size + 2 * tokens * depth * cols
    return pl.pallas_call(
        functools.partial(kernel, n, ntp, local_new, kv_heads, group, slots),
        out_shape=(
            jax.ShapeDtypeStruct((local_new, depth), bf16),
            jax.ShapeDtypeStruct((block, cols), bf16),
        ),
        in_specs=[vmem, hbm, hbm, vmem, vmem, vmem, pl.BlockSpec(memory_space=pltpu.SMEM), hbm],
        out_specs=(vmem, vmem),
        scratch_shapes=[
            pltpu.VMEM((slots * kv_heads, lanes), bf16),
            pltpu.VMEM((slots * kv_heads, lanes), bf16),
            pltpu.VMEM((kv_heads, all_keys, lanes), bf16),
            pltpu.VMEM((kv_heads, all_keys, lanes), bf16),
            pltpu.VMEM((math.gcd(slots, 256) * kv_heads, lanes), f32),
            pltpu.VMEM((new_pad, lanes), f32),
            pltpu.VMEM((1, slots), f32),
            pltpu.VMEM((tokens * group, lanes), f32),
            pltpu.VMEM((tokens, heads, lanes), bf16),
            pltpu.VMEM((depth, cols), bf16),
            pltpu.VMEM((kv_heads, n, rows, lanes), bf16),
            pltpu.VMEM((kv_heads, n, rows, lanes), bf16),
            pltpu.VMEM((kv_heads, chunks, 8, lanes), f32),
            pltpu.VMEM((kv_heads * n * 8, lanes), f32),
            pltpu.VMEM((lanes, n), f32),
            pltpu.VMEM((rows, lanes), f32),
            pltpu.VMEM((kv_heads, n, rows, lanes), bf16),
            pltpu.VMEM((tokens * group, lanes), f32),
            pltpu.VMEM((tokens, group * lanes), bf16),
            pltpu.VMEM((tokens, cols), f32),
            pltpu.VMEM((col_tiles, ntp, 2 * block, half), bf16),
            pltpu.VMEM((col_tiles, ntp, 2 * block, half), bf16),
            dma, dma, dma((4 * kv_heads,)),
            dma((n,)), dma((n,)),
            dma((kv_heads, n)), dma((kv_heads, n)),
            dma((kv_heads, n)), dma((kv_heads, n)),
            dma((kv_heads, n)), dma((kv_heads, n)),
            dma((col_tiles, ntp)), dma((col_tiles, ntp)),
        ],
        compiler_params=pltpu.CompilerParams(
            collective_id=0, has_side_effects=True, vmem_limit_bytes=56 * 2**20
        ),
        cost_estimate=pl.CostEstimate(
            flops=flops,
            bytes_accessed=2 * depth * cols + 4 * slots * kv_heads * head_size,
            transcendentals=tokens * heads * slots,
        ),
    )(
        queries,
        cached_keys.reshape(slots * kv_heads, head_size),
        cached_values.reshape(slots * kv_heads, head_size),
        cached_pos.reshape(1, slots),
        new_keys.reshape(local_new * kv_heads, head_size),
        new_values.reshape(local_new * kv_heads, head_size),
        new_pos,
        out_weight,
    )


def solution(mesh):
    in_specs = (
        P("ctx", "tp", None),
        P("ctx", "tp", None),
        P("ctx", "tp", None),
        P("ctx"),
        P("ctx", "tp", None),
        P("ctx", "tp", None),
        P(),
        P("tp", "ctx"),
    )
    out_specs = (P("ctx", "tp"), P("tp", "ctx"))
    return jax.shard_map(
        functools.partial(per_device, mesh.shape["ctx"], mesh.shape["tp"]),
        mesh=mesh, in_specs=in_specs, out_specs=out_specs, check_vma=False,
    )
```

```python
import functools
import math

import jax
import jax.numpy as jnp
from jax import lax
from jax.experimental import pallas as pl
from jax.experimental.pallas import tpu as pltpu
from jax.sharding import PartitionSpec as P

masked_score = -1e30
MESH = pl.DeviceIdType.MESH
lanes = 128
new_pad = 128
col_tiles = 4
bf16 = jnp.bfloat16
f32 = jnp.float32


def kernel(
    n, ntp, local_new, kv_heads, group, slots,
    q_hbm, k_hbm, v_hbm, pos_hbm, nk_hbm, nv_hbm, newpos_hbm, w_hbm,
    ctx_out, proj_out, pos_ref, nk_ref, nv_ref, newpos_ref,
    kraw, vraw, kh, vh, wide, small, bias_c, bias_n, qall, wbuf,
    onum, rnum, sstat, rstat, wts, cown, call, cf, lhs, acc, dsend, drecv,
    k_sem, v_sem, i_sem, w_sem, q_send, q_recv, n_send, n_recv, s_send, s_recv,
    c_send, c_recv, d_send, d_recv,
):
    me = lax.axis_index("ctx")
    tp = lax.axis_index("tp")
    rows = local_new * group
    per_chunk = lanes // rows
    chunks = n // per_chunk
    mine = me // per_chunk
    tokens = n * local_new
    depth = group * lanes
    coef = math.log2(math.e) / math.sqrt(lanes)

    k_copy = pltpu.make_async_copy(k_hbm, kraw, k_sem)
    v_copy = pltpu.make_async_copy(v_hbm, vraw, v_sem)
    small_copies = [
        pltpu.make_async_copy(src, dst, i_sem.at[i])
        for i, (src, dst) in enumerate(
            [(newpos_hbm, newpos_ref), (pos_hbm, pos_ref), (nk_hbm, nk_ref), (nv_hbm, nv_ref)]
        )
    ]
    own_q = pltpu.make_async_copy(
        q_hbm, qall.at[pl.ds(me * local_new, local_new)], i_sem.at[4]
    )
    for copy in small_copies:
        copy.start()
    own_q.start()
    k_copy.start()
    v_copy.start()
    w_parts = 4 * kv_heads
    w_rows = kv_heads * depth // w_parts
    w_copies = [
        pltpu.make_async_copy(
            w_hbm.at[pl.ds(i * w_rows, w_rows)], wbuf.at[pl.ds(i * w_rows, w_rows)], w_sem.at[i]
        )
        for i in range(w_parts)
    ]

    barrier = pltpu.get_barrier_semaphore()

    def greet(i, _):
        pl.semaphore_signal(
            barrier, inc=1, device_id={"ctx": lax.rem(me + i, n)}, device_id_type=MESH
        )
        return 0

    lax.fori_loop(1, n, greet, 0)
    for i in range(1, ntp):
        pl.semaphore_signal(
            barrier, inc=1, device_id={"tp": lax.rem(tp + i, ntp)}, device_id_type=MESH
        )
    for copy in small_copies:
        copy.wait()
    bias_c[...] = jnp.where(pos_ref[...] >= 0, 0.0, masked_score)
    lane = lax.broadcasted_iota(jnp.int32, (group, lanes), 1)
    key_pos = jnp.full((group, lanes), 2**30, jnp.int32)
    for j in range(local_new):
        key_pos = jnp.where(lane == j, newpos_ref[me * local_new + j], key_pos)

    def mask_new(t, _):
        bias_n[pl.ds(t * group, group), :] = jnp.where(
            key_pos <= newpos_ref[t], 0.0, masked_score
        )
        return 0

    lax.fori_loop(0, tokens, mask_new, 0)

    pl.semaphore_wait(barrier, n - 1 + ntp - 1)

    def q_copy(slot, peer):
        return pltpu.make_async_remote_copy(
            src_ref=q_hbm,
            dst_ref=qall.at[pl.ds(slot * local_new, local_new)],
            send_sem=q_send.at[peer],
            recv_sem=q_recv.at[slot],
            device_id={"ctx": peer},
            device_id_type=MESH,
        )

    def num_copy(h, peer, slot):
        return pltpu.make_async_remote_copy(
            src_ref=onum.at[h, peer],
            dst_ref=rnum.at[h, slot],
            send_sem=n_send.at[h, peer],
            recv_sem=n_recv.at[h, slot],
            device_id={"ctx": peer},
            device_id_type=MESH,
        )

    def stat_copy(h, peer, slot):
        return pltpu.make_async_remote_copy(
            src_ref=sstat.at[h, peer // per_chunk],
            dst_ref=rstat.at[pl.ds((h * n + slot) * 8, 8)],
            send_sem=s_send.at[h, peer],
            recv_sem=s_recv.at[h, slot],
            device_id={"ctx": peer},
            device_id_type=MESH,
        )

    def ctx_copy(h, peer, slot):
        return pltpu.make_async_remote_copy(
            src_ref=call.at[h, slot],
            dst_ref=call.at[h, slot],
            send_sem=c_send.at[h, peer],
            recv_sem=c_recv.at[h, slot],
            device_id={"ctx": peer},
            device_id_type=MESH,
        )

    def part_copy(j, peer, slot):
        return pltpu.make_async_remote_copy(
            src_ref=dsend.at[j, peer],
            dst_ref=drecv.at[j, slot],
            send_sem=d_send.at[j, peer],
            recv_sem=d_recv.at[j, slot],
            device_id={"tp": peer},
            device_id_type=MESH,
        )

    def others(body):
        def step(i, _):
            body(lax.rem(me + i, n))
            return 0

        lax.fori_loop(1, n, step, 0)

    def send_queries(i, _):
        c = lax.rem(mine + chunks - i, chunks)
        for j in range(per_chunk):
            peer = c * per_chunk + j

            @pl.when(peer != me)
            def _():
                q_copy(me, peer).start()

        return 0

    lax.fori_loop(0, chunks, send_queries, 0)

    part = math.gcd(slots, 512)

    def split_heads(raw, new_ref, out):
        def step(i, _):
            wide[...] = raw[pl.ds(i * part * kv_heads, part * kv_heads), :].astype(f32)
            for h in range(kv_heads):
                out[h, pl.ds(i * part, part), :] = wide[
                    pl.ds(h, part, stride=kv_heads), :
                ].astype(bf16)
            return 0

        lax.fori_loop(0, slots // part, step, 0)
        wide[pl.ds(0, local_new * kv_heads), :] = new_ref[...].astype(f32)
        for h in range(kv_heads):
            small[...] = jnp.zeros_like(small)
            small[pl.ds(0, local_new), :] = wide[pl.ds(h, local_new, stride=kv_heads), :]
            out[h, pl.ds(slots, new_pad), :] = small[...].astype(bf16)

    k_copy.wait()
    v_copy.wait()
    for copy in w_copies:
        copy.start()
    split_heads(kraw, nk_ref, kh)
    split_heads(vraw, nv_ref, vh)
    own_q.wait()

    diag = lax.broadcasted_iota(jnp.int32, (lanes, lanes), 0) == lax.broadcasted_iota(
        jnp.int32, (lanes, lanes), 1
    )

    def attend(c, others_of_chunk):
        tok = c * per_chunk * local_new
        for peer in others_of_chunk:
            q_copy(peer, peer).wait_recv()
        scores = []
        for h in range(kv_heads):
            q = qall[pl.ds(tok, per_chunk * local_new), pl.ds(h * group, group), :]
            scores.append(
                lax.dot_general(
                    q.reshape(lanes, lanes), kh[h], (((1,), (1,)), ((), ())),
                    preferred_element_type=f32,
                )
            )
        for h in range(kv_heads):
            s = scores[h]
            old = s[:, :slots] + bias_c[...]
            new = s[:, slots:] + bias_n[pl.ds(tok * group, lanes), :]
            top = jnp.maximum(
                jnp.max(old, axis=1, keepdims=True), jnp.max(new, axis=1, keepdims=True)
            )
            old = jnp.exp2((old - top) * coef)
            new = jnp.exp2((new - top) * coef)
            total = jnp.sum(old, axis=1, keepdims=True) + jnp.sum(new, axis=1, keepdims=True)
            out = jnp.dot(old.astype(bf16), vh[h, :slots], preferred_element_type=f32)
            out += jnp.dot(new.astype(bf16), vh[h, slots:], preferred_element_type=f32)
            out = (out / total).astype(bf16)
            level = top * coef + jnp.log2(total)
            stat = jnp.sum(jnp.where(diag, level, 0.0), axis=0, keepdims=True)
            sstat[h, c] = jnp.broadcast_to(stat, (8, lanes))
            for j in range(per_chunk):
                onum[h, c * per_chunk + j] = out[j * rows : (j + 1) * rows]
        for h in range(kv_heads):
            for peer in others_of_chunk:
                stat_copy(h, peer, me).start()
                num_copy(h, peer, me).start()

    def attend_all():
        attend(
            mine,
            [
                mine * per_chunk + lax.rem(me + j, per_chunk) for j in range(1, per_chunk)
            ],
        )
        for h in range(kv_heads):
            rnum[h, me] = onum[h, me]
            rstat[pl.ds((h * n + me) * 8, 8), :] = sstat[h, mine]

        def step(i, _):
            c = lax.rem(mine + i, chunks)
            attend(c, [c * per_chunk + j for j in range(per_chunk)])
            return 0

        lax.fori_loop(1, chunks, step, 0)

    def combine(h):
        def arrived(peer):
            stat_copy(h, peer, peer).wait_recv()
            num_copy(h, peer, peer).wait_recv()

        others(arrived)
        level = rstat[pl.ds(h * n * 8, n, stride=8), :]
        factor = jnp.exp2(level - jnp.max(level, axis=0, keepdims=True))
        factor = factor / jnp.sum(factor, axis=0, keepdims=True)
        wts[...] = factor.T
        first = pl.multiple_of(lax.rem(me, per_chunk) * rows, rows)
        weight = wts[pl.ds(first, rows), :]
        context = jnp.zeros((rows, lanes), f32)
        for s in range(n):
            context += rnum[h, s].astype(f32) * weight[:, s : s + 1]
        call[h, me] = context.astype(bf16)
        others(lambda peer: ctx_copy(h, peer, me).start())
        cown[...] = context
        for g in range(group):
            at = (h * group + g) * lanes
            ctx_out[:, at : at + lanes] = cown[pl.ds(g, local_new, stride=group), :].astype(bf16)

    tile = proj_out.shape[1] // col_tiles
    half = tile // 2
    block = tokens // ntp

    def project(h):
        others(lambda peer: ctx_copy(h, peer, peer).wait_recv())
        cf[...] = call[h].reshape(tokens * group, lanes).astype(f32)
        for g in range(group):
            lhs[:, g * lanes : (g + 1) * lanes] = cf[pl.ds(g, tokens, stride=group), :].astype(bf16)
        for copy in w_copies[h * 4 : (h + 1) * 4]:
            copy.wait()
        for j in range(col_tiles):
            cols = slice(j * tile, (j + 1) * tile)
            term = jnp.dot(
                lhs[...], wbuf[h * depth : (h + 1) * depth, cols], preferred_element_type=f32
            )
            if h > 0:
                term += acc[:, cols]
            if h < kv_heads - 1:
                acc[:, cols] = term
                continue
            for r in range(ntp):
                slab = term[r * block : (r + 1) * block]
                slab = jnp.concatenate([slab[:, :half], slab[:, half:]], axis=0).astype(bf16)
                dsend[j, r] = slab

                @pl.when(tp != r)
                def _():
                    part_copy(j, r, tp).start()

                @pl.when(tp == r)
                def _():
                    drecv[j, tp] = slab

    attend_all()
    for h in range(kv_heads):
        combine(h)
    for h in range(kv_heads):
        project(h)

    for j in range(col_tiles):
        for i in range(1, ntp):
            peer = lax.rem(tp + i, ntp)
            part_copy(j, peer, peer).wait_recv()
        total = drecv[j, 0].astype(f32)
        for r in range(1, ntp):
            total += drecv[j, r].astype(f32)
        proj_out[:, j * tile : (j + 1) * tile] = jnp.concatenate(
            [total[:block], total[block:]], axis=1
        ).astype(bf16)

    def sent(peer):
        q_copy(me, peer).wait_send()
        for h in range(kv_heads):
            num_copy(h, peer, me).wait_send()
            stat_copy(h, peer, me).wait_send()
            ctx_copy(h, peer, me).wait_send()

    others(sent)
    for j in range(col_tiles):
        for i in range(1, ntp):
            part_copy(j, lax.rem(tp + i, ntp), tp).wait_send()


def deliver(ctx_in, proj_in, ctx_out, proj_out, sem):
    copies = [
        pltpu.make_async_copy(ctx_in, ctx_out, sem.at[0]),
        pltpu.make_async_copy(proj_in, proj_out, sem.at[1]),
    ]
    for copy in copies:
        copy.start()
    for copy in copies:
        copy.wait()


def per_device(
    n, ntp, queries, cached_keys, cached_values, cached_pos, new_keys, new_values, new_pos,
    out_weight,
):
    local_new, heads, head_size = queries.shape
    slots, kv_heads = cached_keys.shape[:2]
    group = heads // kv_heads
    rows = local_new * group
    tokens = n * local_new
    depth, cols = out_weight.shape
    chunks = n // (lanes // rows)
    all_keys = slots + new_pad
    block = tokens // ntp
    half = cols // col_tiles // 2
    vmem = pl.BlockSpec(memory_space=pltpu.VMEM)
    hbm = pl.BlockSpec(memory_space=pl.ANY)
    dma = pltpu.SemaphoreType.DMA
    flops = 4 * tokens * heads * slots * head_size + 2 * tokens * depth * cols
    out_shape = (
            jax.ShapeDtypeStruct((local_new, depth), bf16),
            jax.ShapeDtypeStruct((block, cols), bf16),
        )
    context, projected = pl.pallas_call(
        functools.partial(kernel, n, ntp, local_new, kv_heads, group, slots),
        out_shape=out_shape,
        in_specs=[hbm] * 8,
        out_specs=(vmem, vmem),
        scratch_shapes=[
            pltpu.VMEM((1, slots), jnp.int32),
            pltpu.VMEM((local_new * kv_heads, lanes), bf16),
            pltpu.VMEM((local_new * kv_heads, lanes), bf16),
            pltpu.SMEM((tokens,), jnp.int32),
            pltpu.VMEM((slots * kv_heads, lanes), bf16),
            pltpu.VMEM((slots * kv_heads, lanes), bf16),
            pltpu.VMEM((kv_heads, all_keys, lanes), bf16),
            pltpu.VMEM((kv_heads, all_keys, lanes), bf16),
            pltpu.VMEM((math.gcd(slots, 512) * kv_heads, lanes), f32),
            pltpu.VMEM((new_pad, lanes), f32),
            pltpu.VMEM((1, slots), f32),
            pltpu.VMEM((tokens * group, lanes), f32),
            pltpu.VMEM((tokens, heads, lanes), bf16),
            pltpu.VMEM((depth, cols), bf16),
            pltpu.VMEM((kv_heads, n, rows, lanes), bf16),
            pltpu.VMEM((kv_heads, n, rows, lanes), bf16),
            pltpu.VMEM((kv_heads, chunks, 8, lanes), f32),
            pltpu.VMEM((kv_heads * n * 8, lanes), f32),
            pltpu.VMEM((lanes, n), f32),
            pltpu.VMEM((rows, lanes), f32),
            pltpu.VMEM((kv_heads, n, rows, lanes), bf16),
            pltpu.VMEM((tokens * group, lanes), f32),
            pltpu.VMEM((tokens, group * lanes), bf16),
            pltpu.VMEM((tokens, cols), f32),
            pltpu.VMEM((col_tiles, ntp, 2 * block, half), bf16),
            pltpu.VMEM((col_tiles, ntp, 2 * block, half), bf16),
            dma, dma, dma((5,)), dma((4 * kv_heads,)),
            dma((n,)), dma((n,)),
            dma((kv_heads, n)), dma((kv_heads, n)),
            dma((kv_heads, n)), dma((kv_heads, n)),
            dma((kv_heads, n)), dma((kv_heads, n)),
            dma((col_tiles, ntp)), dma((col_tiles, ntp)),
        ],
        compiler_params=pltpu.CompilerParams(
            collective_id=0, has_side_effects=True, vmem_limit_bytes=56 * 2**20
        ),
        cost_estimate=pl.CostEstimate(
            flops=flops,
            bytes_accessed=2 * depth * cols + 4 * slots * kv_heads * head_size,
            transcendentals=tokens * heads * slots,
        ),
    )(
        queries,
        cached_keys.reshape(slots * kv_heads, head_size),
        cached_values.reshape(slots * kv_heads, head_size),
        cached_pos.reshape(1, slots),
        new_keys.reshape(local_new * kv_heads, head_size),
        new_values.reshape(local_new * kv_heads, head_size),
        new_pos,
        out_weight,
    )
    return pl.pallas_call(
        deliver,
        out_shape=out_shape,
        in_specs=[hbm, hbm],
        out_specs=(hbm, hbm),
        scratch_shapes=[dma((2,))],
        compiler_params=pltpu.CompilerParams(vmem_limit_bytes=60 * 2**20),
    )(context, projected)


def solution(mesh):
    in_specs = (
        P("ctx", "tp", None),
        P("ctx", "tp", None),
        P("ctx", "tp", None),
        P("ctx"),
        P("ctx", "tp", None),
        P("ctx", "tp", None),
        P(),
        P("tp", "ctx"),
    )
    out_specs = (P("ctx", "tp"), P("tp", "ctx"))
    return jax.shard_map(
        functools.partial(per_device, mesh.shape["ctx"], mesh.shape["tp"]),
        mesh=mesh, in_specs=in_specs, out_specs=out_specs, check_vma=False,
    )
```

```python
import functools
import math

import jax
import jax.numpy as jnp
from jax import lax
from jax.experimental import pallas as pl
from jax.experimental.pallas import tpu as pltpu
from jax.sharding import PartitionSpec as P

masked_score = -1e30
MESH = pl.DeviceIdType.MESH
lanes = 128
new_pad = 128
col_tiles = 4
bf16 = jnp.bfloat16
f32 = jnp.float32


def kernel(
    n, ntp, local_new, kv_heads, group, slots,
    q_hbm, k_hbm, v_hbm, pos_hbm, nk_hbm, nv_hbm, newpos_hbm, w_hbm,
    ctx_out, proj_out, pos_ref, nk_ref, nv_ref, newpos_ref,
    kraw, vraw, kh, vh, wide, small, bias_c, bias_n, qall, wbuf,
    onum, rnum, sstat, rstat, wts, cown, call, cf, lhs, acc, dsend, drecv,
    k_sem, v_sem, i_sem, w_sem, q_send, q_recv, n_send, n_recv, s_send, s_recv,
    c_send, c_recv, d_send, d_recv,
):
    me = lax.axis_index("ctx")
    tp = lax.axis_index("tp")
    rows = local_new * group
    per_chunk = lanes // rows
    chunks = n // per_chunk
    mine = me // per_chunk
    outer = n // 2
    hi = me // 2
    lo = lax.rem(me, 2)
    mate = hi * 2 + 1 - lo
    tokens = n * local_new
    depth = group * lanes
    coef = math.log2(math.e) / math.sqrt(lanes)

    k_copy = pltpu.make_async_copy(k_hbm, kraw, k_sem)
    v_copy = pltpu.make_async_copy(v_hbm, vraw, v_sem)
    small_copies = [
        pltpu.make_async_copy(src, dst, i_sem.at[i])
        for i, (src, dst) in enumerate(
            [(newpos_hbm, newpos_ref), (pos_hbm, pos_ref), (nk_hbm, nk_ref), (nv_hbm, nv_ref)]
        )
    ]
    own_q = pltpu.make_async_copy(
        q_hbm, qall.at[pl.ds(me * local_new, local_new)], i_sem.at[4]
    )
    for copy in small_copies:
        copy.start()
    own_q.start()
    k_copy.start()
    v_copy.start()
    w_parts = 4 * kv_heads
    w_rows = kv_heads * depth // w_parts
    w_copies = [
        pltpu.make_async_copy(
            w_hbm.at[pl.ds(i * w_rows, w_rows)], wbuf.at[pl.ds(i * w_rows, w_rows)], w_sem.at[i]
        )
        for i in range(w_parts)
    ]

    barrier = pltpu.get_barrier_semaphore()

    def greet(i, _):
        pl.semaphore_signal(
            barrier, inc=1, device_id={"ctx": lax.rem(me + i, n)}, device_id_type=MESH
        )
        return 0

    lax.fori_loop(1, n, greet, 0)
    for i in range(1, ntp):
        pl.semaphore_signal(
            barrier, inc=1, device_id={"tp": lax.rem(tp + i, ntp)}, device_id_type=MESH
        )
    for copy in small_copies:
        copy.wait()
    bias_c[...] = jnp.where(pos_ref[...] >= 0, 0.0, masked_score)
    lane = lax.broadcasted_iota(jnp.int32, (group, lanes), 1)
    key_pos = jnp.full((group, lanes), 2**30, jnp.int32)
    for j in range(local_new):
        key_pos = jnp.where(lane == j, newpos_ref[me * local_new + j], key_pos)

    def mask_new(t, _):
        bias_n[pl.ds(t * group, group), :] = jnp.where(
            key_pos <= newpos_ref[t], 0.0, masked_score
        )
        return 0

    lax.fori_loop(0, tokens, mask_new, 0)

    pl.semaphore_wait(barrier, n - 1 + ntp - 1)

    def q_copy(slot, peer, sem):
        part = qall.at[pl.ds(slot * local_new, local_new)]
        return pltpu.make_async_remote_copy(
            src_ref=part,
            dst_ref=part,
            send_sem=q_send.at[sem],
            recv_sem=q_recv.at[slot],
            device_id={"ctx": peer},
            device_id_type=MESH,
        )

    def num_copy(h, peer, slot):
        return pltpu.make_async_remote_copy(
            src_ref=onum.at[h, peer],
            dst_ref=rnum.at[h, slot],
            send_sem=n_send.at[h, peer],
            recv_sem=n_recv.at[h, slot],
            device_id={"ctx": peer},
            device_id_type=MESH,
        )

    def stat_copy(h, peer, slot):
        return pltpu.make_async_remote_copy(
            src_ref=sstat.at[h, peer // per_chunk],
            dst_ref=rstat.at[pl.ds((h * n + slot) * 8, 8)],
            send_sem=s_send.at[h, peer],
            recv_sem=s_recv.at[h, slot],
            device_id={"ctx": peer},
            device_id_type=MESH,
        )

    def ctx_copy(h, peer, slot, sem):
        return pltpu.make_async_remote_copy(
            src_ref=call.at[h, slot],
            dst_ref=call.at[h, slot],
            send_sem=c_send.at[h, sem],
            recv_sem=c_recv.at[h, slot],
            device_id={"ctx": peer},
            device_id_type=MESH,
        )

    def part_copy(j, peer, slot):
        return pltpu.make_async_remote_copy(
            src_ref=dsend.at[j, peer],
            dst_ref=drecv.at[j, slot],
            send_sem=d_send.at[j, peer],
            recv_sem=d_recv.at[j, slot],
            device_id={"tp": peer},
            device_id_type=MESH,
        )

    def others(body):
        def step(i, _):
            body(lax.rem(me + i, n))
            return 0

        lax.fori_loop(1, n, step, 0)

    def peers(first, last, body):
        def step(i, _):
            body(lax.rem(hi + i, outer) * 2 + lo)
            return 0

        lax.fori_loop(first, last, step, 0)

    own_q.wait()
    q_copy(me, mate, mate).start()
    peers(1, outer, lambda peer: q_copy(me, peer, peer).start())

    def pass_queries(slot):
        q_copy(slot, slot, slot).wait_recv()
        q_copy(slot, mate, slot + 1 - 2 * lo).start()

    part = math.gcd(slots, 512)

    def split_heads(raw, new_ref, out):
        def step(i, _):
            wide[...] = raw[pl.ds(i * part * kv_heads, part * kv_heads), :].astype(f32)
            for h in range(kv_heads):
                out[h, pl.ds(i * part, part), :] = wide[
                    pl.ds(h, part, stride=kv_heads), :
                ].astype(bf16)
            return 0

        lax.fori_loop(0, slots // part, step, 0)
        wide[pl.ds(0, local_new * kv_heads), :] = new_ref[...].astype(f32)
        for h in range(kv_heads):
            small[...] = jnp.zeros_like(small)
            small[pl.ds(0, local_new), :] = wide[pl.ds(h, local_new, stride=kv_heads), :]
            out[h, pl.ds(slots, new_pad), :] = small[...].astype(bf16)

    k_copy.wait()
    v_copy.wait()
    for copy in w_copies:
        copy.start()
    split_heads(kraw, nk_ref, kh)
    peers(outer - 1, outer, pass_queries)
    split_heads(vraw, nv_ref, vh)
    peers(1, outer - 1, pass_queries)

    diag = lax.broadcasted_iota(jnp.int32, (lanes, lanes), 0) == lax.broadcasted_iota(
        jnp.int32, (lanes, lanes), 1
    )

    def attend(c, others_of_chunk):
        tok = c * per_chunk * local_new
        if per_chunk % 2 == 0:
            for j in range(per_chunk // 2):
                slot = c * per_chunk + 2 * j + 1 - lo
                q_copy(slot, slot, slot).wait_recv()
        else:

            @pl.when(lax.rem(c, 2) != lo)
            def _():
                q_copy(c, c, c).wait_recv()

        scores = []
        for h in range(kv_heads):
            q = qall[pl.ds(tok, per_chunk * local_new), pl.ds(h * group, group), :]
            scores.append(
                lax.dot_general(
                    q.reshape(lanes, lanes), kh[h], (((1,), (1,)), ((), ())),
                    preferred_element_type=f32,
                )
            )
        for h in range(kv_heads):
            s = scores[h]
            old = s[:, :slots] + bias_c[...]
            new = s[:, slots:] + bias_n[pl.ds(tok * group, lanes), :]
            top = jnp.maximum(
                jnp.max(old, axis=1, keepdims=True), jnp.max(new, axis=1, keepdims=True)
            )
            old = jnp.exp2((old - top) * coef)
            new = jnp.exp2((new - top) * coef)
            total = jnp.sum(old, axis=1, keepdims=True) + jnp.sum(new, axis=1, keepdims=True)
            out = jnp.dot(old.astype(bf16), vh[h, :slots], preferred_element_type=f32)
            out += jnp.dot(new.astype(bf16), vh[h, slots:], preferred_element_type=f32)
            out = (out / total).astype(bf16)
            level = top * coef + jnp.log2(total)
            stat = jnp.sum(jnp.where(diag, level, 0.0), axis=0, keepdims=True)
            sstat[h, c] = jnp.broadcast_to(stat, (8, lanes))
            for j in range(per_chunk):
                onum[h, c * per_chunk + j] = out[j * rows : (j + 1) * rows]
        for h in range(kv_heads):
            for peer in others_of_chunk:
                stat_copy(h, peer, me).start()
                num_copy(h, peer, me).start()

    def attend_all():
        attend(
            mine,
            [
                mine * per_chunk + lax.rem(me + j, per_chunk) for j in range(1, per_chunk)
            ],
        )
        for h in range(kv_heads):
            rnum[h, me] = onum[h, me]
            rstat[pl.ds((h * n + me) * 8, 8), :] = sstat[h, mine]

        def step(i, _):
            c = lax.rem(mine + chunks - i, chunks)
            attend(c, [c * per_chunk + j for j in range(per_chunk)])
            return 0

        lax.fori_loop(1, chunks, step, 0)

    def combine(h):
        def arrived(peer):
            stat_copy(h, peer, peer).wait_recv()
            num_copy(h, peer, peer).wait_recv()

        others(arrived)
        level = rstat[pl.ds(h * n * 8, n, stride=8), :]
        factor = jnp.exp2(level - jnp.max(level, axis=0, keepdims=True))
        factor = factor / jnp.sum(factor, axis=0, keepdims=True)
        wts[...] = factor.T
        first = pl.multiple_of(lax.rem(me, per_chunk) * rows, rows)
        weight = wts[pl.ds(first, rows), :]
        context = jnp.zeros((rows, lanes), f32)
        for s in range(n):
            context += rnum[h, s].astype(f32) * weight[:, s : s + 1]
        call[h, me] = context.astype(bf16)
        peers(1, outer, lambda peer: ctx_copy(h, peer, me, peer).start())
        ctx_copy(h, mate, me, mate).start()
        cown[...] = context
        for g in range(group):
            at = (h * group + g) * lanes
            ctx_out[:, at : at + lanes] = cown[pl.ds(g, local_new, stride=group), :].astype(bf16)

    def relay(h):
        def body(slot):
            ctx_copy(h, slot, slot, slot).wait_recv()
            ctx_copy(h, mate, slot, slot + 1 - 2 * lo).start()

        peers(1, outer, body)

    tile = proj_out.shape[1] // col_tiles
    half = tile // 2
    block = tokens // ntp

    def project(h):
        def from_mate(i, _):
            slot = i * 2 + 1 - lo
            ctx_copy(h, slot, slot, slot).wait_recv()
            return 0

        lax.fori_loop(0, outer, from_mate, 0)
        cf[...] = call[h].reshape(tokens * group, lanes).astype(f32)
        for g in range(group):
            lhs[:, g * lanes : (g + 1) * lanes] = cf[pl.ds(g, tokens, stride=group), :].astype(bf16)
        for copy in w_copies[h * 4 : (h + 1) * 4]:
            copy.wait()
        for j in range(col_tiles):
            cols = slice(j * tile, (j + 1) * tile)
            term = jnp.dot(
                lhs[...], wbuf[h * depth : (h + 1) * depth, cols], preferred_element_type=f32
            )
            if h > 0:
                term += acc[:, cols]
            if h < kv_heads - 1:
                acc[:, cols] = term
                continue
            for r in range(ntp):
                slab = term[r * block : (r + 1) * block]
                slab = jnp.concatenate([slab[:, :half], slab[:, half:]], axis=0).astype(bf16)
                dsend[j, r] = slab

                @pl.when(tp != r)
                def _():
                    part_copy(j, r, tp).start()

                @pl.when(tp == r)
                def _():
                    drecv[j, tp] = slab

    attend_all()
    for h in range(kv_heads):
        combine(h)
    for h in range(kv_heads):
        relay(h)
    for h in range(kv_heads):
        project(h)

    for j in range(col_tiles):
        for i in range(1, ntp):
            peer = lax.rem(tp + i, ntp)
            part_copy(j, peer, peer).wait_recv()
        total = drecv[j, 0].astype(f32)
        for r in range(1, ntp):
            total += drecv[j, r].astype(f32)
        proj_out[:, j * tile : (j + 1) * tile] = jnp.concatenate(
            [total[:block], total[block:]], axis=1
        ).astype(bf16)

    def sent(peer):
        q_copy(me, peer, peer).wait_send()
        for h in range(kv_heads):
            num_copy(h, peer, me).wait_send()
            stat_copy(h, peer, me).wait_send()
            ctx_copy(h, peer, me, peer).wait_send()

    others(sent)
    for j in range(col_tiles):
        for i in range(1, ntp):
            part_copy(j, lax.rem(tp + i, ntp), tp).wait_send()


def deliver(ctx_in, proj_in, ctx_out, proj_out):
    ctx_out[...] = ctx_in[...]
    proj_out[...] = proj_in[...]


def per_device(
    n, ntp, queries, cached_keys, cached_values, cached_pos, new_keys, new_values, new_pos,
    out_weight,
):
    local_new, heads, head_size = queries.shape
    slots, kv_heads = cached_keys.shape[:2]
    group = heads // kv_heads
    rows = local_new * group
    tokens = n * local_new
    depth, cols = out_weight.shape
    chunks = n // (lanes // rows)
    all_keys = slots + new_pad
    block = tokens // ntp
    half = cols // col_tiles // 2
    vmem = pl.BlockSpec(memory_space=pltpu.VMEM)
    hbm = pl.BlockSpec(memory_space=pl.ANY)
    dma = pltpu.SemaphoreType.DMA
    flops = 4 * tokens * heads * slots * head_size + 2 * tokens * depth * cols
    out_shape = (
            jax.ShapeDtypeStruct((local_new, depth), bf16),
            jax.ShapeDtypeStruct((block, cols), bf16),
        )
    context, projected = pl.pallas_call(
        functools.partial(kernel, n, ntp, local_new, kv_heads, group, slots),
        out_shape=out_shape,
        in_specs=[hbm] * 8,
        out_specs=(vmem, vmem),
        scratch_shapes=[
            pltpu.VMEM((1, slots), jnp.int32),
            pltpu.VMEM((local_new * kv_heads, lanes), bf16),
            pltpu.VMEM((local_new * kv_heads, lanes), bf16),
            pltpu.SMEM((tokens,), jnp.int32),
            pltpu.VMEM((slots * kv_heads, lanes), bf16),
            pltpu.VMEM((slots * kv_heads, lanes), bf16),
            pltpu.VMEM((kv_heads, all_keys, lanes), bf16),
            pltpu.VMEM((kv_heads, all_keys, lanes), bf16),
            pltpu.VMEM((math.gcd(slots, 512) * kv_heads, lanes), f32),
            pltpu.VMEM((new_pad, lanes), f32),
            pltpu.VMEM((1, slots), f32),
            pltpu.VMEM((tokens * group, lanes), f32),
            pltpu.VMEM((tokens, heads, lanes), bf16),
            pltpu.VMEM((depth, cols), bf16),
            pltpu.VMEM((kv_heads, n, rows, lanes), bf16),
            pltpu.VMEM((kv_heads, n, rows, lanes), bf16),
            pltpu.VMEM((kv_heads, chunks, 8, lanes), f32),
            pltpu.VMEM((kv_heads * n * 8, lanes), f32),
            pltpu.VMEM((lanes, n), f32),
            pltpu.VMEM((rows, lanes), f32),
            pltpu.VMEM((kv_heads, n, rows, lanes), bf16),
            pltpu.VMEM((tokens * group, lanes), f32),
            pltpu.VMEM((tokens, group * lanes), bf16),
            pltpu.VMEM((tokens, cols), f32),
            pltpu.VMEM((col_tiles, ntp, 2 * block, half), bf16),
            pltpu.VMEM((col_tiles, ntp, 2 * block, half), bf16),
            dma, dma, dma((5,)), dma((4 * kv_heads,)),
            dma((n,)), dma((n,)),
            dma((kv_heads, n)), dma((kv_heads, n)),
            dma((kv_heads, n)), dma((kv_heads, n)),
            dma((kv_heads, n)), dma((kv_heads, n)),
            dma((col_tiles, ntp)), dma((col_tiles, ntp)),
        ],
        compiler_params=pltpu.CompilerParams(
            collective_id=0, has_side_effects=True, vmem_limit_bytes=56 * 2**20
        ),
        cost_estimate=pl.CostEstimate(
            flops=flops,
            bytes_accessed=2 * depth * cols + 4 * slots * kv_heads * head_size,
            transcendentals=tokens * heads * slots,
        ),
    )(
        queries,
        cached_keys.reshape(slots * kv_heads, head_size),
        cached_values.reshape(slots * kv_heads, head_size),
        cached_pos.reshape(1, slots),
        new_keys.reshape(local_new * kv_heads, head_size),
        new_values.reshape(local_new * kv_heads, head_size),
        new_pos,
        out_weight,
    )
    return pl.pallas_call(
        deliver,
        out_shape=out_shape,
        in_specs=[vmem, vmem],
        out_specs=(vmem, vmem),
    )(context, projected)


def solution(mesh):
    in_specs = (
        P("ctx", "tp", None),
        P("ctx", "tp", None),
        P("ctx", "tp", None),
        P("ctx"),
        P("ctx", "tp", None),
        P("ctx", "tp", None),
        P(),
        P("tp", "ctx"),
    )
    out_specs = (P("ctx", "tp"), P("tp", "ctx"))
    return jax.shard_map(
        functools.partial(per_device, mesh.shape["ctx"], mesh.shape["tp"]),
        mesh=mesh, in_specs=in_specs, out_specs=out_specs, check_vma=False,
    )
```

```python
import functools
import math

import jax
import jax.numpy as jnp
from jax import lax
from jax.experimental import pallas as pl
from jax.experimental.pallas import tpu as pltpu
from jax.sharding import PartitionSpec as P

masked_score = -1e30
MESH = pl.DeviceIdType.MESH
lanes = 128
new_pad = 128
col_tiles = 2
stat_rows = 16
bf16 = jnp.bfloat16
f32 = jnp.float32


def kernel(
    n, ntp, local_new, kv_heads, group, slots,
    q_hbm, k_hbm, v_hbm, pos_hbm, nk_hbm, nv_hbm, newpos_hbm, w_hbm,
    ctx_out, proj_out, pos_ref, nk_ref, nv_ref, newpos_ref,
    kraw, vraw, kh, vh, wide, small, bias_c, bias_n, qall, wbuf,
    onum, rnum, stat, wts, cown, call, cf, lhs, acc, dsend, drecv,
    k_sem, v_sem, i_sem, w_sem, q_send, q_recv, n_send, n_recv,
    c_send, c_recv, d_send, d_recv,
):
    me = lax.axis_index("ctx")
    tp = lax.axis_index("tp")
    rows = local_new * group
    per_chunk = lanes // rows
    chunks = n // per_chunk
    mine = me // per_chunk
    num_rows = kv_heads * rows
    tokens = n * local_new
    depth = group * lanes
    coef = math.log2(math.e) / math.sqrt(lanes)

    k_copy = pltpu.make_async_copy(k_hbm, kraw, k_sem)
    v_copy = pltpu.make_async_copy(v_hbm, vraw, v_sem)
    small_copies = [
        pltpu.make_async_copy(src, dst, i_sem.at[i])
        for i, (src, dst) in enumerate(
            [(newpos_hbm, newpos_ref), (pos_hbm, pos_ref), (nk_hbm, nk_ref), (nv_hbm, nv_ref)]
        )
    ]
    own_q = pltpu.make_async_copy(
        q_hbm, qall.at[pl.ds(me * local_new, local_new)], i_sem.at[4]
    )
    for copy in small_copies:
        copy.start()
    own_q.start()
    k_copy.start()
    v_copy.start()
    w_parts = 4 * kv_heads
    w_rows = kv_heads * depth // w_parts
    w_copies = [
        pltpu.make_async_copy(
            w_hbm.at[pl.ds(i * w_rows, w_rows)], wbuf.at[pl.ds(i * w_rows, w_rows)], w_sem.at[i]
        )
        for i in range(w_parts)
    ]

    barrier = pltpu.get_barrier_semaphore()

    def greet(i, _):
        pl.semaphore_signal(
            barrier, inc=1, device_id={"ctx": lax.rem(me + i, n)}, device_id_type=MESH
        )
        return 0

    lax.fori_loop(1, n, greet, 0)
    for i in range(1, ntp):
        pl.semaphore_signal(
            barrier, inc=1, device_id={"tp": lax.rem(tp + i, ntp)}, device_id_type=MESH
        )
    for copy in small_copies:
        copy.wait()
    bias_c[...] = jnp.where(pos_ref[...] >= 0, 0.0, masked_score)
    lane = lax.broadcasted_iota(jnp.int32, (group, lanes), 1)
    key_pos = jnp.full((group, lanes), 2**30, jnp.int32)
    for j in range(local_new):
        key_pos = jnp.where(lane == j, newpos_ref[me * local_new + j], key_pos)

    def mask_new(t, _):
        bias_n[pl.ds(t * group, group), :] = jnp.where(
            key_pos <= newpos_ref[t], 0.0, masked_score
        )
        return 0

    lax.fori_loop(0, tokens, mask_new, 0)

    pl.semaphore_wait(barrier, n - 1 + ntp - 1)

    def q_copy(peer):
        return pltpu.make_async_remote_copy(
            src_ref=q_hbm,
            dst_ref=qall.at[pl.ds(me * local_new, local_new)],
            send_sem=q_send,
            recv_sem=q_recv.at[mine],
            device_id={"ctx": peer},
            device_id_type=MESH,
        )

    def num_copy(peer):
        return pltpu.make_async_remote_copy(
            src_ref=onum.at[peer],
            dst_ref=rnum.at[me],
            send_sem=n_send,
            recv_sem=n_recv,
            device_id={"ctx": peer},
            device_id_type=MESH,
        )

    def ctx_copy(h, peer):
        return pltpu.make_async_remote_copy(
            src_ref=call.at[h, me],
            dst_ref=call.at[h, me],
            send_sem=c_send.at[h],
            recv_sem=c_recv.at[h],
            device_id={"ctx": peer},
            device_id_type=MESH,
        )

    def part_copy(j, peer):
        return pltpu.make_async_remote_copy(
            src_ref=dsend.at[j, peer],
            dst_ref=drecv.at[j, tp],
            send_sem=d_send.at[j],
            recv_sem=d_recv.at[j],
            device_id={"tp": peer},
            device_id_type=MESH,
        )

    def await_bytes(ref, sem):
        pltpu.make_async_copy(ref, ref, sem).wait()

    def others(body):
        def step(i, _):
            body(lax.rem(me + i, n))
            return 0

        lax.fori_loop(1, n, step, 0)

    def chunk_at(i, sign):
        shift = lax.rem(i + chunks // 2 - 2, chunks - 1) + 1
        return lax.rem(mine + chunks + sign * shift, chunks)

    for j in range(1, per_chunk):
        q_copy(mine * per_chunk + lax.rem(me + j, per_chunk)).start()

    def send_queries(i, _):
        c = chunk_at(i, 1)
        for j in range(per_chunk):
            q_copy(c * per_chunk + j).start()
        return 0

    lax.fori_loop(1, chunks, send_queries, 0)

    part = math.gcd(slots, 512)

    def split_heads(raw, new_ref, out):
        def step(i, _):
            wide[...] = raw[pl.ds(i * part * kv_heads, part * kv_heads), :].astype(f32)
            for h in range(kv_heads):
                out[h, pl.ds(i * part, part), :] = wide[
                    pl.ds(h, part, stride=kv_heads), :
                ].astype(bf16)
            return 0

        lax.fori_loop(0, slots // part, step, 0)
        wide[pl.ds(0, local_new * kv_heads), :] = new_ref[...].astype(f32)
        for h in range(kv_heads):
            small[...] = jnp.zeros_like(small)
            small[pl.ds(0, local_new), :] = wide[pl.ds(h, local_new, stride=kv_heads), :]
            out[h, pl.ds(slots, new_pad), :] = small[...].astype(bf16)

    k_copy.wait()
    v_copy.wait()
    for copy in w_copies:
        copy.start()
    split_heads(kraw, nk_ref, kh)
    split_heads(vraw, nv_ref, vh)
    own_q.wait()

    stat_row = lax.broadcasted_iota(jnp.int32, (stat_rows, lanes), 0)
    diag = lax.broadcasted_iota(jnp.int32, (lanes, lanes), 0) == lax.broadcasted_iota(
        jnp.int32, (lanes, lanes), 1
    )

    def attend(c, others_of_chunk):
        tok = c * per_chunk * local_new
        arrivals = len(others_of_chunk) * local_new
        if arrivals > 0:
            await_bytes(qall.at[pl.ds(0, arrivals)], q_recv.at[c])
        scores = []
        for h in range(kv_heads):
            q = qall[pl.ds(tok, per_chunk * local_new), pl.ds(h * group, group), :]
            scores.append(
                lax.dot_general(
                    q.reshape(lanes, lanes), kh[h], (((1,), (1,)), ((), ())),
                    preferred_element_type=f32,
                )
            )
        levels = jnp.zeros((stat_rows, lanes), f32)
        for h in range(kv_heads):
            s = scores[h]
            old = s[:, :slots] + bias_c[...]
            new = s[:, slots:] + bias_n[pl.ds(tok * group, lanes), :]
            top = jnp.maximum(
                jnp.max(old, axis=1, keepdims=True), jnp.max(new, axis=1, keepdims=True)
            )
            old = jnp.exp2((old - top) * coef)
            new = jnp.exp2((new - top) * coef)
            total = jnp.sum(old, axis=1, keepdims=True) + jnp.sum(new, axis=1, keepdims=True)
            out = jnp.dot(old.astype(bf16), vh[h, :slots], preferred_element_type=f32)
            out += jnp.dot(new.astype(bf16), vh[h, slots:], preferred_element_type=f32)
            out = (out / total).astype(bf16)
            level = top * coef + jnp.log2(total)
            level = jnp.sum(jnp.where(diag, level, 0.0), axis=0, keepdims=True)
            for k in range(3):
                piece = level.astype(bf16).astype(f32)
                level = level - piece
                levels = jnp.where(stat_row == 3 * h + k, piece, levels)
            for j in range(per_chunk):
                onum[c * per_chunk + j, h * rows : (h + 1) * rows] = out[
                    j * rows : (j + 1) * rows
                ]
        for j in range(per_chunk):
            onum[c * per_chunk + j, num_rows:] = levels.astype(bf16)
        for peer in others_of_chunk:
            num_copy(peer).start()

    def attend_all():
        attend(
            mine,
            [
                mine * per_chunk + lax.rem(me + j, per_chunk) for j in range(1, per_chunk)
            ],
        )
        rnum[me] = onum[me]

        def step(i, _):
            c = chunk_at(i, -1)
            attend(c, [c * per_chunk + j for j in range(per_chunk)])
            return 0

        lax.fori_loop(1, chunks, step, 0)

    def combine(h):
        level = stat[pl.ds(3 * h, n, stride=stat_rows), :]
        for k in range(1, 3):
            level += stat[pl.ds(3 * h + k, n, stride=stat_rows), :]
        factor = jnp.exp2(level - jnp.max(level, axis=0, keepdims=True))
        factor = factor / jnp.sum(factor, axis=0, keepdims=True)
        wts[...] = factor.T
        first = pl.multiple_of(lax.rem(me, per_chunk) * rows, rows)
        weight = wts[pl.ds(first, rows), :]
        context = jnp.zeros((rows, lanes), f32)
        for s in range(n):
            context += rnum[s, h * rows : (h + 1) * rows].astype(f32) * weight[:, s : s + 1]
        call[h, me] = context.astype(bf16)
        others(lambda peer: ctx_copy(h, peer).start())
        cown[...] = context
        for g in range(group):
            at = (h * group + g) * lanes
            ctx_out[:, at : at + lanes] = cown[pl.ds(g, local_new, stride=group), :].astype(bf16)

    tile = proj_out.shape[1] // col_tiles
    half = tile // 2
    block = tokens // ntp

    def project(h):
        await_bytes(call.at[h, pl.ds(0, n - 1)], c_recv.at[h])
        cf[...] = call[h].reshape(tokens * group, lanes).astype(f32)
        for g in range(group):
            lhs[:, g * lanes : (g + 1) * lanes] = cf[pl.ds(g, tokens, stride=group), :].astype(bf16)
        for copy in w_copies[h * 4 : (h + 1) * 4]:
            copy.wait()
        for j in range(col_tiles):
            cols = slice(j * tile, (j + 1) * tile)
            term = jnp.dot(
                lhs[...], wbuf[h * depth : (h + 1) * depth, cols], preferred_element_type=f32
            )
            if h > 0:
                term += acc[:, cols]
            if h < kv_heads - 1:
                acc[:, cols] = term
                continue
            for r in range(ntp):
                slab = term[r * block : (r + 1) * block]
                slab = jnp.concatenate([slab[:, :half], slab[:, half:]], axis=0).astype(bf16)
                dsend[j, r] = slab

                @pl.when(tp != r)
                def _():
                    part_copy(j, r).start()

                @pl.when(tp == r)
                def _():
                    drecv[j, tp] = slab

    attend_all()
    await_bytes(rnum.at[pl.ds(0, n - 1)], n_recv)
    stat[...] = rnum[:, num_rows:, :].reshape(n * stat_rows, lanes).astype(f32)
    for h in range(kv_heads):
        combine(h)
    for h in range(kv_heads):
        project(h)

    for j in range(col_tiles):
        await_bytes(drecv.at[j, pl.ds(0, ntp - 1)], d_recv.at[j])
        total = drecv[j, 0].astype(f32)
        for r in range(1, ntp):
            total += drecv[j, r].astype(f32)
        proj_out[:, j * tile : (j + 1) * tile] = jnp.concatenate(
            [total[:block], total[block:]], axis=1
        ).astype(bf16)

    await_bytes(qall.at[pl.ds(0, (n - 1) * local_new)], q_send)
    await_bytes(onum.at[pl.ds(0, n - 1)], n_send)
    for h in range(kv_heads):
        await_bytes(call.at[h, pl.ds(0, n - 1)], c_send.at[h])
    for j in range(col_tiles):
        await_bytes(dsend.at[j, pl.ds(0, ntp - 1)], d_send.at[j])


def deliver(ctx_in, proj_in, ctx_out, proj_out):
    ctx_out[...] = ctx_in[...]
    proj_out[...] = proj_in[...]


def per_device(
    n, ntp, queries, cached_keys, cached_values, cached_pos, new_keys, new_values, new_pos,
    out_weight,
):
    local_new, heads, head_size = queries.shape
    slots, kv_heads = cached_keys.shape[:2]
    group = heads // kv_heads
    rows = local_new * group
    tokens = n * local_new
    depth, cols = out_weight.shape
    chunks = n // (lanes // rows)
    all_keys = slots + new_pad
    block = tokens // ntp
    half = cols // col_tiles // 2
    vmem = pl.BlockSpec(memory_space=pltpu.VMEM)
    hbm = pl.BlockSpec(memory_space=pl.ANY)
    dma = pltpu.SemaphoreType.DMA
    flops = 4 * tokens * heads * slots * head_size + 2 * tokens * depth * cols
    out_shape = (
            jax.ShapeDtypeStruct((local_new, depth), bf16),
            jax.ShapeDtypeStruct((block, cols), bf16),
        )
    context, projected = pl.pallas_call(
        functools.partial(kernel, n, ntp, local_new, kv_heads, group, slots),
        out_shape=out_shape,
        in_specs=[hbm] * 8,
        out_specs=(vmem, vmem),
        scratch_shapes=[
            pltpu.VMEM((1, slots), jnp.int32),
            pltpu.VMEM((local_new * kv_heads, lanes), bf16),
            pltpu.VMEM((local_new * kv_heads, lanes), bf16),
            pltpu.SMEM((tokens,), jnp.int32),
            pltpu.VMEM((slots * kv_heads, lanes), bf16),
            pltpu.VMEM((slots * kv_heads, lanes), bf16),
            pltpu.VMEM((kv_heads, all_keys, lanes), bf16),
            pltpu.VMEM((kv_heads, all_keys, lanes), bf16),
            pltpu.VMEM((math.gcd(slots, 512) * kv_heads, lanes), f32),
            pltpu.VMEM((new_pad, lanes), f32),
            pltpu.VMEM((1, slots), f32),
            pltpu.VMEM((tokens * group, lanes), f32),
            pltpu.VMEM((tokens, heads, lanes), bf16),
            pltpu.VMEM((depth, cols), bf16),
            pltpu.VMEM((n, kv_heads * rows + stat_rows, lanes), bf16),
            pltpu.VMEM((n, kv_heads * rows + stat_rows, lanes), bf16),
            pltpu.VMEM((n * stat_rows, lanes), f32),
            pltpu.VMEM((lanes, n), f32),
            pltpu.VMEM((rows, lanes), f32),
            pltpu.VMEM((kv_heads, n, rows, lanes), bf16),
            pltpu.VMEM((tokens * group, lanes), f32),
            pltpu.VMEM((tokens, group * lanes), bf16),
            pltpu.VMEM((tokens, cols), f32),
            pltpu.VMEM((col_tiles, ntp, 2 * block, half), bf16),
            pltpu.VMEM((col_tiles, ntp, 2 * block, half), bf16),
            dma, dma, dma((5,)), dma((4 * kv_heads,)),
            dma, dma((chunks,)), dma, dma,
            dma((kv_heads,)), dma((kv_heads,)), dma((col_tiles,)), dma((col_tiles,)),
        ],
        compiler_params=pltpu.CompilerParams(
            collective_id=0, has_side_effects=True, vmem_limit_bytes=56 * 2**20
        ),
        cost_estimate=pl.CostEstimate(
            flops=flops,
            bytes_accessed=2 * depth * cols + 4 * slots * kv_heads * head_size,
            transcendentals=tokens * heads * slots,
        ),
    )(
        queries,
        cached_keys.reshape(slots * kv_heads, head_size),
        cached_values.reshape(slots * kv_heads, head_size),
        cached_pos.reshape(1, slots),
        new_keys.reshape(local_new * kv_heads, head_size),
        new_values.reshape(local_new * kv_heads, head_size),
        new_pos,
        out_weight,
    )
    return pl.pallas_call(
        deliver,
        out_shape=out_shape,
        in_specs=[vmem, vmem],
        out_specs=(vmem, vmem),
    )(context, projected)


def solution(mesh):
    in_specs = (
        P("ctx", "tp", None),
        P("ctx", "tp", None),
        P("ctx", "tp", None),
        P("ctx"),
        P("ctx", "tp", None),
        P("ctx", "tp", None),
        P(),
        P("tp", "ctx"),
    )
    out_specs = (P("ctx", "tp"), P("tp", "ctx"))
    return jax.shard_map(
        functools.partial(per_device, mesh.shape["ctx"], mesh.shape["tp"]),
        mesh=mesh, in_specs=in_specs, out_specs=out_specs, check_vma=False,
    )
```

```python
import functools
import math

import jax
import jax.numpy as jnp
from jax import lax
from jax.experimental import pallas as pl
from jax.experimental.pallas import tpu as pltpu
from jax.sharding import PartitionSpec as P

masked_score = -1e30
MESH = pl.DeviceIdType.MESH
lanes = 128
new_pad = 128
col_tiles = 2
stat_rows = 16
bf16 = jnp.bfloat16
f32 = jnp.float32


def kernel(
    n, ntp, local_new, kv_heads, group, slots,
    q_hbm, k_hbm, v_hbm, pos_hbm, nk_hbm, nv_hbm, newpos_hbm, w_hbm,
    ctx_out, proj_out, pos_ref, nk_ref, nv_ref, newpos_ref,
    kraw, vraw, kh, vh, wide, small, bias_c, bias_n, qall, wbuf,
    sbuf, pbuf, onum, rnum, stat, wts, cown, call, cf, lhs, acc, dsend, drecv,
    k_sem, v_sem, i_sem, w_sem, q_send, q_recv, n_send, n_recv,
    c_send, c_recv, d_send, d_recv,
):
    me = lax.axis_index("ctx")
    tp = lax.axis_index("tp")
    rows = local_new * group
    per_chunk = lanes // rows
    chunks = n // per_chunk
    mine = me // per_chunk
    num_rows = kv_heads * rows
    tokens = n * local_new
    depth = group * lanes
    coef = math.log2(math.e) / math.sqrt(lanes)

    k_copy = pltpu.make_async_copy(k_hbm, kraw, k_sem)
    v_copy = pltpu.make_async_copy(v_hbm, vraw, v_sem)
    small_copies = [
        pltpu.make_async_copy(src, dst, i_sem.at[i])
        for i, (src, dst) in enumerate(
            [(newpos_hbm, newpos_ref), (pos_hbm, pos_ref), (nk_hbm, nk_ref), (nv_hbm, nv_ref)]
        )
    ]
    own_q = pltpu.make_async_copy(
        q_hbm, qall.at[pl.ds(me * local_new, local_new)], i_sem.at[4]
    )
    for copy in small_copies:
        copy.start()
    own_q.start()
    k_copy.start()
    v_copy.start()
    w_parts = 4 * kv_heads
    w_rows = kv_heads * depth // w_parts
    w_copies = [
        pltpu.make_async_copy(
            w_hbm.at[pl.ds(i * w_rows, w_rows)], wbuf.at[pl.ds(i * w_rows, w_rows)], w_sem.at[i]
        )
        for i in range(w_parts)
    ]

    barrier = pltpu.get_barrier_semaphore()

    def greet(i, _):
        pl.semaphore_signal(
            barrier, inc=1, device_id={"ctx": lax.rem(me + i, n)}, device_id_type=MESH
        )
        return 0

    lax.fori_loop(1, n, greet, 0)
    for i in range(1, ntp):
        pl.semaphore_signal(
            barrier, inc=1, device_id={"tp": lax.rem(tp + i, ntp)}, device_id_type=MESH
        )
    for copy in small_copies:
        copy.wait()
    bias_c[...] = jnp.where(pos_ref[...] >= 0, 0.0, masked_score)
    lane = lax.broadcasted_iota(jnp.int32, (group, lanes), 1)
    key_pos = jnp.full((group, lanes), 2**30, jnp.int32)
    for j in range(local_new):
        key_pos = jnp.where(lane == j, newpos_ref[me * local_new + j], key_pos)

    def mask_new(t, _):
        bias_n[pl.ds(t * group, group), :] = jnp.where(
            key_pos <= newpos_ref[t], 0.0, masked_score
        )
        return 0

    lax.fori_loop(0, tokens, mask_new, 0)

    pl.semaphore_wait(barrier, n - 1 + ntp - 1)

    def q_copy(peer):
        return pltpu.make_async_remote_copy(
            src_ref=q_hbm,
            dst_ref=qall.at[pl.ds(me * local_new, local_new)],
            send_sem=q_send,
            recv_sem=q_recv.at[mine],
            device_id={"ctx": peer},
            device_id_type=MESH,
        )

    def num_copy(peer):
        return pltpu.make_async_remote_copy(
            src_ref=onum.at[peer],
            dst_ref=rnum.at[me],
            send_sem=n_send,
            recv_sem=n_recv,
            device_id={"ctx": peer},
            device_id_type=MESH,
        )

    def ctx_copy(h, peer):
        return pltpu.make_async_remote_copy(
            src_ref=call.at[h, me],
            dst_ref=call.at[h, me],
            send_sem=c_send.at[h],
            recv_sem=c_recv.at[h],
            device_id={"ctx": peer},
            device_id_type=MESH,
        )

    def part_copy(j, peer):
        return pltpu.make_async_remote_copy(
            src_ref=dsend.at[j, peer],
            dst_ref=drecv.at[j, tp],
            send_sem=d_send.at[j],
            recv_sem=d_recv.at[j],
            device_id={"tp": peer},
            device_id_type=MESH,
        )

    def await_bytes(ref, sem):
        pltpu.make_async_copy(ref, ref, sem).wait()

    def others(body):
        def step(i, _):
            body(lax.rem(me + i, n))
            return 0

        lax.fori_loop(1, n, step, 0)

    def chunk_at(i, sign):
        shift = lax.rem(i + chunks // 2 - 2 + chunks - 1, chunks - 1) + 1
        return lax.rem(mine + chunks + sign * shift, chunks)

    for j in range(1, per_chunk):
        q_copy(mine * per_chunk + lax.rem(me + j, per_chunk)).start()

    def send_queries(i, _):
        c = chunk_at(i, 1)
        for j in range(per_chunk):
            q_copy(c * per_chunk + j).start()
        return 0

    lax.fori_loop(1, chunks, send_queries, 0)

    part = math.gcd(slots, 512)

    def split_heads(raw, new_ref, out):
        def step(i, _):
            wide[...] = raw[pl.ds(i * part * kv_heads, part * kv_heads), :].astype(f32)
            for h in range(kv_heads):
                out[h, pl.ds(i * part, part), :] = wide[
                    pl.ds(h, part, stride=kv_heads), :
                ].astype(bf16)
            return 0

        lax.fori_loop(0, slots // part, step, 0)
        wide[pl.ds(0, local_new * kv_heads), :] = new_ref[...].astype(f32)
        for h in range(kv_heads):
            small[...] = jnp.zeros_like(small)
            small[pl.ds(0, local_new), :] = wide[pl.ds(h, local_new, stride=kv_heads), :]
            out[h, pl.ds(slots, new_pad), :] = small[...].astype(bf16)

    k_copy.wait()
    v_copy.wait()
    for copy in w_copies:
        copy.start()
    split_heads(kraw, nk_ref, kh)
    split_heads(vraw, nv_ref, vh)
    own_q.wait()

    stat_row = lax.broadcasted_iota(jnp.int32, (stat_rows, lanes), 0)
    diag = lax.broadcasted_iota(jnp.int32, (lanes, lanes), 0) == lax.broadcasted_iota(
        jnp.int32, (lanes, lanes), 1
    )

    def fold(old, new, op):
        first = op(old[:, :lanes], new)
        return jnp.concatenate([first, old[:, lanes:]], axis=1)

    def attend(c):
        tok = c * per_chunk * local_new
        for h in range(kv_heads):
            q = qall[pl.ds(tok, per_chunk * local_new), pl.ds(h * group, group), :]
            sbuf[h] = lax.dot_general(
                q.reshape(lanes, lanes), kh[h], (((1,), (1,)), ((), ())),
                preferred_element_type=f32,
            )
        levels = jnp.zeros((stat_rows, lanes), f32)
        blocks = lanes // 16
        for h in range(kv_heads):

            def masked(b):
                at = pl.ds(b * 16, 16)
                old = sbuf[h, at, :slots] + bias_c[...]
                new = sbuf[h, at, slots:] + bias_n[pl.ds(tok * group + b * 16, 16), :]
                return old, new

            tops = []
            for b in range(blocks):
                tops.append(jnp.max(fold(*masked(b), jnp.maximum), axis=1, keepdims=True))
            totals = []
            for b in range(blocks):
                old, new = masked(b)
                old = jnp.exp2((old - tops[b]) * coef)
                new = jnp.exp2((new - tops[b]) * coef)
                totals.append(jnp.sum(fold(old, new, jnp.add), axis=1, keepdims=True))
                pbuf[h, b * 16 : (b + 1) * 16, :slots] = old.astype(bf16)
                pbuf[h, b * 16 : (b + 1) * 16, slots:] = new.astype(bf16)
            top = jnp.concatenate(tops, axis=0)
            total = jnp.concatenate(totals, axis=0)
            out = jnp.dot(pbuf[h], vh[h], preferred_element_type=f32)
            out = (out / total).astype(bf16)
            level = top * coef + jnp.log2(total)
            level = jnp.sum(jnp.where(diag, level, 0.0), axis=0, keepdims=True)
            for k in range(3):
                piece = level.astype(bf16).astype(f32)
                level = level - piece
                levels = jnp.where(stat_row == 3 * h + k, piece, levels)
            for j in range(per_chunk):
                onum[c * per_chunk + j, h * rows : (h + 1) * rows] = out[
                    j * rows : (j + 1) * rows
                ]
        for j in range(per_chunk):
            onum[c * per_chunk + j, num_rows:] = levels.astype(bf16)

    def attend_all():
        def step(i, _):
            c = jnp.where(i == 0, mine, chunk_at(i, -1))

            @pl.when(i > 0)
            def _():
                await_bytes(qall.at[pl.ds(0, per_chunk * local_new)], q_recv.at[c])

            if per_chunk > 1:

                @pl.when(i == 0)
                def _():
                    await_bytes(qall.at[pl.ds(0, (per_chunk - 1) * local_new)], q_recv.at[c])

            attend(c)

            @pl.when(i > 0)
            def _():
                for j in range(per_chunk):
                    num_copy(c * per_chunk + j).start()

            @pl.when(i == 0)
            def _():
                for j in range(1, per_chunk):
                    num_copy(c * per_chunk + lax.rem(me + j, per_chunk)).start()
                rnum[me] = onum[me]

            return 0

        lax.fori_loop(0, chunks, step, 0)

    def combine(h):
        level = stat[pl.ds(3 * h, n, stride=stat_rows), :]
        for k in range(1, 3):
            level += stat[pl.ds(3 * h + k, n, stride=stat_rows), :]
        factor = jnp.exp2(level - jnp.max(level, axis=0, keepdims=True))
        factor = factor / jnp.sum(factor, axis=0, keepdims=True)
        wts[...] = factor.T
        first = pl.multiple_of(lax.rem(me, per_chunk) * rows, rows)
        weight = wts[pl.ds(first, rows), :]
        context = jnp.zeros((rows, lanes), f32)
        for s in range(n):
            context += rnum[s, h * rows : (h + 1) * rows].astype(f32) * weight[:, s : s + 1]
        call[h, me] = context.astype(bf16)
        others(lambda peer: ctx_copy(h, peer).start())
        cown[...] = context
        for g in range(group):
            at = (h * group + g) * lanes
            ctx_out[:, at : at + lanes] = cown[pl.ds(g, local_new, stride=group), :].astype(bf16)

    tile = proj_out.shape[1] // col_tiles
    half = tile // 2
    block = tokens // ntp

    def project(h):
        await_bytes(call.at[h, pl.ds(0, n - 1)], c_recv.at[h])
        cf[...] = call[h].reshape(tokens * group, lanes).astype(f32)
        for g in range(group):
            lhs[:, g * lanes : (g + 1) * lanes] = cf[pl.ds(g, tokens, stride=group), :].astype(bf16)
        for copy in w_copies[h * 4 : (h + 1) * 4]:
            copy.wait()
        for j in range(col_tiles):
            cols = slice(j * tile, (j + 1) * tile)
            term = jnp.dot(
                lhs[...], wbuf[h * depth : (h + 1) * depth, cols], preferred_element_type=f32
            )
            if h > 0:
                term += acc[:, cols]
            if h < kv_heads - 1:
                acc[:, cols] = term
                continue
            for r in range(ntp):
                slab = term[r * block : (r + 1) * block]
                slab = jnp.concatenate([slab[:, :half], slab[:, half:]], axis=0).astype(bf16)
                dsend[j, r] = slab

                @pl.when(tp != r)
                def _():
                    part_copy(j, r).start()

                @pl.when(tp == r)
                def _():
                    drecv[j, tp] = slab

    attend_all()
    await_bytes(rnum.at[pl.ds(0, n - 1)], n_recv)
    stat[...] = rnum[:, num_rows:, :].reshape(n * stat_rows, lanes).astype(f32)
    for h in range(kv_heads):
        combine(h)
    for h in range(kv_heads):
        project(h)

    for j in range(col_tiles):
        await_bytes(drecv.at[j, pl.ds(0, ntp - 1)], d_recv.at[j])
        total = drecv[j, 0].astype(f32)
        for r in range(1, ntp):
            total += drecv[j, r].astype(f32)
        proj_out[:, j * tile : (j + 1) * tile] = jnp.concatenate(
            [total[:block], total[block:]], axis=1
        ).astype(bf16)

    await_bytes(qall.at[pl.ds(0, (n - 1) * local_new)], q_send)
    await_bytes(onum.at[pl.ds(0, n - 1)], n_send)
    for h in range(kv_heads):
        await_bytes(call.at[h, pl.ds(0, n - 1)], c_send.at[h])
    for j in range(col_tiles):
        await_bytes(dsend.at[j, pl.ds(0, ntp - 1)], d_send.at[j])


def deliver(ctx_in, proj_in, ctx_out, proj_out):
    ctx_out[...] = ctx_in[...]
    proj_out[...] = proj_in[...]


def per_device(
    n, ntp, queries, cached_keys, cached_values, cached_pos, new_keys, new_values, new_pos,
    out_weight,
):
    local_new, heads, head_size = queries.shape
    slots, kv_heads = cached_keys.shape[:2]
    group = heads // kv_heads
    rows = local_new * group
    tokens = n * local_new
    depth, cols = out_weight.shape
    chunks = n // (lanes // rows)
    all_keys = slots + new_pad
    block = tokens // ntp
    half = cols // col_tiles // 2
    vmem = pl.BlockSpec(memory_space=pltpu.VMEM)
    hbm = pl.BlockSpec(memory_space=pl.ANY)
    dma = pltpu.SemaphoreType.DMA
    flops = 4 * tokens * heads * slots * head_size + 2 * tokens * depth * cols
    out_shape = (
            jax.ShapeDtypeStruct((local_new, depth), bf16),
            jax.ShapeDtypeStruct((block, cols), bf16),
        )
    context, projected = pl.pallas_call(
        functools.partial(kernel, n, ntp, local_new, kv_heads, group, slots),
        out_shape=out_shape,
        in_specs=[hbm] * 8,
        out_specs=(vmem, vmem),
        scratch_shapes=[
            pltpu.VMEM((1, slots), jnp.int32),
            pltpu.VMEM((local_new * kv_heads, lanes), bf16),
            pltpu.VMEM((local_new * kv_heads, lanes), bf16),
            pltpu.SMEM((tokens,), jnp.int32),
            pltpu.VMEM((slots * kv_heads, lanes), bf16),
            pltpu.VMEM((slots * kv_heads, lanes), bf16),
            pltpu.VMEM((kv_heads, all_keys, lanes), bf16),
            pltpu.VMEM((kv_heads, all_keys, lanes), bf16),
            pltpu.VMEM((math.gcd(slots, 512) * kv_heads, lanes), f32),
            pltpu.VMEM((new_pad, lanes), f32),
            pltpu.VMEM((1, slots), f32),
            pltpu.VMEM((tokens * group, lanes), f32),
            pltpu.VMEM((tokens, heads, lanes), bf16),
            pltpu.VMEM((depth, cols), bf16),
            pltpu.VMEM((kv_heads, lanes, all_keys), f32),
            pltpu.VMEM((kv_heads, lanes, all_keys), bf16),
            pltpu.VMEM((n, kv_heads * rows + stat_rows, lanes), bf16),
            pltpu.VMEM((n, kv_heads * rows + stat_rows, lanes), bf16),
            pltpu.VMEM((n * stat_rows, lanes), f32),
            pltpu.VMEM((lanes, n), f32),
            pltpu.VMEM((rows, lanes), f32),
            pltpu.VMEM((kv_heads, n, rows, lanes), bf16),
            pltpu.VMEM((tokens * group, lanes), f32),
            pltpu.VMEM((tokens, group * lanes), bf16),
            pltpu.VMEM((tokens, cols), f32),
            pltpu.VMEM((col_tiles, ntp, 2 * block, half), bf16),
            pltpu.VMEM((col_tiles, ntp, 2 * block, half), bf16),
            dma, dma, dma((5,)), dma((4 * kv_heads,)),
            dma, dma((chunks,)), dma, dma,
            dma((kv_heads,)), dma((kv_heads,)), dma((col_tiles,)), dma((col_tiles,)),
        ],
        compiler_params=pltpu.CompilerParams(
            collective_id=0, has_side_effects=True, vmem_limit_bytes=56 * 2**20
        ),
        cost_estimate=pl.CostEstimate(
            flops=flops,
            bytes_accessed=2 * depth * cols + 4 * slots * kv_heads * head_size,
            transcendentals=tokens * heads * slots,
        ),
    )(
        queries,
        cached_keys.reshape(slots * kv_heads, head_size),
        cached_values.reshape(slots * kv_heads, head_size),
        cached_pos.reshape(1, slots),
        new_keys.reshape(local_new * kv_heads, head_size),
        new_values.reshape(local_new * kv_heads, head_size),
        new_pos,
        out_weight,
    )
    return pl.pallas_call(
        deliver,
        out_shape=out_shape,
        in_specs=[vmem, vmem],
        out_specs=(vmem, vmem),
    )(context, projected)


def solution(mesh):
    in_specs = (
        P("ctx", "tp", None),
        P("ctx", "tp", None),
        P("ctx", "tp", None),
        P("ctx"),
        P("ctx", "tp", None),
        P("ctx", "tp", None),
        P(),
        P("tp", "ctx"),
    )
    out_specs = (P("ctx", "tp"), P("tp", "ctx"))
    return jax.shard_map(
        functools.partial(per_device, mesh.shape["ctx"], mesh.shape["tp"]),
        mesh=mesh, in_specs=in_specs, out_specs=out_specs, check_vma=False,
    )
```

```python
import functools
import math

import jax
import jax.numpy as jnp
from jax import lax
from jax.experimental import pallas as pl
from jax.experimental.pallas import tpu as pltpu
from jax.sharding import PartitionSpec as P

masked_score = -1e30
MESH = pl.DeviceIdType.MESH
lanes = 128
new_pad = 128
col_tiles = 2
stat_rows = 16
bf16 = jnp.bfloat16
f32 = jnp.float32


def kernel(
    n, ntp, local_new, kv_heads, group, slots,
    q_hbm, k_hbm, v_hbm, pos_hbm, nk_hbm, nv_hbm, newpos_hbm, w_hbm,
    ctx_out, proj_out, pos_ref, nk_ref, nv_ref, newpos_ref,
    kraw, vraw, kh, vh, wide, small, bias_c, bias_n, qall, wbuf,
    onum, rnum, stat, wts, cown, call, cf, lhs, acc, dsend, drecv,
    k_sem, v_sem, i_sem, w_sem, q_send, q_recv, n_send, n_recv,
    c_send, c_recv, d_send, d_recv,
):
    me = lax.axis_index("ctx")
    tp = lax.axis_index("tp")
    rows = local_new * group
    per_chunk = lanes // rows
    chunks = n // per_chunk
    mine = me // per_chunk
    tokens = n * local_new
    depth = group * lanes
    coef = math.log2(math.e) / math.sqrt(lanes)

    k_copy = pltpu.make_async_copy(k_hbm, kraw, k_sem)
    v_copy = pltpu.make_async_copy(v_hbm, vraw, v_sem)
    small_copies = [
        pltpu.make_async_copy(src, dst, i_sem.at[i])
        for i, (src, dst) in enumerate(
            [(newpos_hbm, newpos_ref), (pos_hbm, pos_ref), (nk_hbm, nk_ref), (nv_hbm, nv_ref)]
        )
    ]
    own_q = pltpu.make_async_copy(
        q_hbm, qall.at[pl.ds(me * local_new, local_new)], i_sem.at[4]
    )
    for copy in small_copies:
        copy.start()
    own_q.start()
    k_copy.start()
    v_copy.start()
    w_parts = 4 * kv_heads
    w_rows = kv_heads * depth // w_parts
    w_copies = [
        pltpu.make_async_copy(
            w_hbm.at[pl.ds(i * w_rows, w_rows)], wbuf.at[pl.ds(i * w_rows, w_rows)], w_sem.at[i]
        )
        for i in range(w_parts)
    ]

    barrier = pltpu.get_barrier_semaphore()

    def greet(i, _):
        pl.semaphore_signal(
            barrier, inc=1, device_id={"ctx": lax.rem(me + i, n)}, device_id_type=MESH
        )
        return 0

    lax.fori_loop(1, n, greet, 0)
    for i in range(1, ntp):
        pl.semaphore_signal(
            barrier, inc=1, device_id={"tp": lax.rem(tp + i, ntp)}, device_id_type=MESH
        )
    for copy in small_copies:
        copy.wait()
    bias_c[...] = jnp.where(pos_ref[...] >= 0, 0.0, masked_score)
    lane = lax.broadcasted_iota(jnp.int32, (group, lanes), 1)
    key_pos = jnp.full((group, lanes), 2**30, jnp.int32)
    for j in range(local_new):
        key_pos = jnp.where(lane == j, newpos_ref[me * local_new + j], key_pos)

    def mask_new(t, _):
        bias_n[pl.ds(t * group, group), :] = jnp.where(
            key_pos <= newpos_ref[t], 0.0, masked_score
        )
        return 0

    lax.fori_loop(0, tokens, mask_new, 0)

    pl.semaphore_wait(barrier, n - 1 + ntp - 1)

    def q_copy(h, peer):
        heads = pl.ds(h * group, group)
        return pltpu.make_async_remote_copy(
            src_ref=q_hbm.at[:, heads],
            dst_ref=qall.at[pl.ds(me * local_new, local_new), heads],
            send_sem=q_send,
            recv_sem=q_recv.at[h, mine],
            device_id={"ctx": peer},
            device_id_type=MESH,
        )

    def num_copy(h, peer):
        return pltpu.make_async_remote_copy(
            src_ref=onum.at[h, peer],
            dst_ref=rnum.at[h, me],
            send_sem=n_send.at[h],
            recv_sem=n_recv.at[h],
            device_id={"ctx": peer},
            device_id_type=MESH,
        )

    def ctx_copy(h, peer):
        return pltpu.make_async_remote_copy(
            src_ref=call.at[h, me],
            dst_ref=call.at[h, me],
            send_sem=c_send.at[h],
            recv_sem=c_recv.at[h],
            device_id={"ctx": peer},
            device_id_type=MESH,
        )

    def part_copy(j, peer):
        return pltpu.make_async_remote_copy(
            src_ref=dsend.at[j, peer],
            dst_ref=drecv.at[j, tp],
            send_sem=d_send.at[j],
            recv_sem=d_recv.at[j],
            device_id={"tp": peer},
            device_id_type=MESH,
        )

    def await_bytes(ref, sem):
        pltpu.make_async_copy(ref, ref, sem).wait()

    def others(body):
        def step(i, _):
            body(lax.rem(me + i, n))
            return 0

        lax.fori_loop(1, n, step, 0)

    def chunk_at(i, sign):
        shift = lax.rem(i + chunks // 2 - 2, chunks - 1) + 1
        return lax.rem(mine + chunks + sign * shift, chunks)

    for h in range(kv_heads):
        for j in range(1, per_chunk):
            q_copy(h, mine * per_chunk + lax.rem(me + j, per_chunk)).start()

        def send_queries(i, _):
            c = chunk_at(i, 1)
            for j in range(per_chunk):
                q_copy(h, c * per_chunk + j).start()
            return 0

        lax.fori_loop(1, chunks, send_queries, 0)

    part = math.gcd(slots, 512)

    def split_heads(raw, new_ref, out):
        def step(i, _):
            wide[...] = raw[pl.ds(i * part * kv_heads, part * kv_heads), :].astype(f32)
            for h in range(kv_heads):
                out[h, pl.ds(i * part, part), :] = wide[
                    pl.ds(h, part, stride=kv_heads), :
                ].astype(bf16)
            return 0

        lax.fori_loop(0, slots // part, step, 0)
        wide[pl.ds(0, local_new * kv_heads), :] = new_ref[...].astype(f32)
        for h in range(kv_heads):
            small[...] = jnp.zeros_like(small)
            small[pl.ds(0, local_new), :] = wide[pl.ds(h, local_new, stride=kv_heads), :]
            out[h, pl.ds(slots, new_pad), :] = small[...].astype(bf16)

    k_copy.wait()
    v_copy.wait()
    for copy in w_copies:
        copy.start()
    split_heads(kraw, nk_ref, kh)
    split_heads(vraw, nv_ref, vh)
    own_q.wait()

    stat_row = lax.broadcasted_iota(jnp.int32, (stat_rows, lanes), 0)
    diag = lax.broadcasted_iota(jnp.int32, (lanes, lanes), 0) == lax.broadcasted_iota(
        jnp.int32, (lanes, lanes), 1
    )

    def attend(h, c, others_of_chunk):
        tok = c * per_chunk * local_new
        heads = pl.ds(h * group, group)
        arrivals = len(others_of_chunk) * local_new
        if arrivals > 0:
            await_bytes(qall.at[pl.ds(0, arrivals), heads], q_recv.at[h, c])
        q = qall[pl.ds(tok, per_chunk * local_new), heads, :].reshape(lanes, lanes)
        s = lax.dot_general(
            q, kh[h], (((1,), (1,)), ((), ())), preferred_element_type=f32
        )
        old = s[:, :slots] + bias_c[...]
        new = s[:, slots:] + bias_n[pl.ds(tok * group, lanes), :]
        top = jnp.maximum(
            jnp.max(old, axis=1, keepdims=True), jnp.max(new, axis=1, keepdims=True)
        )
        old = jnp.exp2((old - top) * coef)
        new = jnp.exp2((new - top) * coef)
        total = jnp.sum(old, axis=1, keepdims=True) + jnp.sum(new, axis=1, keepdims=True)
        out = jnp.dot(old.astype(bf16), vh[h, :slots], preferred_element_type=f32)
        out += jnp.dot(new.astype(bf16), vh[h, slots:], preferred_element_type=f32)
        out = (out / total).astype(bf16)
        level = top * coef + jnp.log2(total)
        level = jnp.sum(jnp.where(diag, level, 0.0), axis=0, keepdims=True)
        levels = jnp.zeros((stat_rows, lanes), f32)
        for k in range(3):
            piece = level.astype(bf16).astype(f32)
            level = level - piece
            levels = jnp.where(stat_row == k, piece, levels)
        for j in range(per_chunk):
            onum[h, c * per_chunk + j, :rows] = out[j * rows : (j + 1) * rows]
            onum[h, c * per_chunk + j, rows:] = levels.astype(bf16)
        for peer in others_of_chunk:
            num_copy(h, peer).start()

    def attend_all(h):
        attend(
            h, mine,
            [
                mine * per_chunk + lax.rem(me + j, per_chunk) for j in range(1, per_chunk)
            ],
        )
        rnum[h, me] = onum[h, me]

        def step(i, _):
            c = chunk_at(i, -1)
            attend(h, c, [c * per_chunk + j for j in range(per_chunk)])
            return 0

        lax.fori_loop(1, chunks, step, 0)

    def combine(h):
        await_bytes(rnum.at[h, pl.ds(0, n - 1)], n_recv.at[h])
        stat[...] = rnum[h, :, rows:, :].reshape(n * stat_rows, lanes).astype(f32)
        level = stat[pl.ds(0, n, stride=stat_rows), :]
        for k in range(1, 3):
            level += stat[pl.ds(k, n, stride=stat_rows), :]
        factor = jnp.exp2(level - jnp.max(level, axis=0, keepdims=True))
        factor = factor / jnp.sum(factor, axis=0, keepdims=True)
        wts[...] = factor.T
        first = pl.multiple_of(lax.rem(me, per_chunk) * rows, rows)
        weight = wts[pl.ds(first, rows), :]
        context = jnp.zeros((rows, lanes), f32)
        for s in range(n):
            context += rnum[h, s, :rows].astype(f32) * weight[:, s : s + 1]
        call[h, me] = context.astype(bf16)
        others(lambda peer: ctx_copy(h, peer).start())
        cown[...] = context
        for g in range(group):
            at = (h * group + g) * lanes
            ctx_out[:, at : at + lanes] = cown[pl.ds(g, local_new, stride=group), :].astype(bf16)

    tile = proj_out.shape[1] // col_tiles
    half = tile // 2
    block = tokens // ntp

    def project(h):
        await_bytes(call.at[h, pl.ds(0, n - 1)], c_recv.at[h])
        cf[...] = call[h].reshape(tokens * group, lanes).astype(f32)
        for g in range(group):
            lhs[:, g * lanes : (g + 1) * lanes] = cf[pl.ds(g, tokens, stride=group), :].astype(bf16)
        for copy in w_copies[h * 4 : (h + 1) * 4]:
            copy.wait()
        for j in range(col_tiles):
            cols = slice(j * tile, (j + 1) * tile)
            term = jnp.dot(
                lhs[...], wbuf[h * depth : (h + 1) * depth, cols], preferred_element_type=f32
            )
            if h > 0:
                term += acc[:, cols]
            if h < kv_heads - 1:
                acc[:, cols] = term
                continue
            for r in range(ntp):
                slab = term[r * block : (r + 1) * block]
                slab = jnp.concatenate([slab[:, :half], slab[:, half:]], axis=0).astype(bf16)
                dsend[j, r] = slab

                @pl.when(tp != r)
                def _():
                    part_copy(j, r).start()

                @pl.when(tp == r)
                def _():
                    drecv[j, tp] = slab

    for h in range(kv_heads):
        attend_all(h)
    for h in range(kv_heads):
        combine(h)
    for h in range(kv_heads):
        project(h)

    for j in range(col_tiles):
        await_bytes(drecv.at[j, pl.ds(0, ntp - 1)], d_recv.at[j])
        total = drecv[j, 0].astype(f32)
        for r in range(1, ntp):
            total += drecv[j, r].astype(f32)
        proj_out[:, j * tile : (j + 1) * tile] = jnp.concatenate(
            [total[:block], total[block:]], axis=1
        ).astype(bf16)

    await_bytes(qall.at[pl.ds(0, (n - 1) * local_new)], q_send)
    for h in range(kv_heads):
        await_bytes(onum.at[h, pl.ds(0, n - 1)], n_send.at[h])
        await_bytes(call.at[h, pl.ds(0, n - 1)], c_send.at[h])
    for j in range(col_tiles):
        await_bytes(dsend.at[j, pl.ds(0, ntp - 1)], d_send.at[j])


def deliver(ctx_in, proj_in, ctx_out, proj_out):
    ctx_out[...] = ctx_in[...]
    proj_out[...] = proj_in[...]


def per_device(
    n, ntp, queries, cached_keys, cached_values, cached_pos, new_keys, new_values, new_pos,
    out_weight,
):
    local_new, heads, head_size = queries.shape
    slots, kv_heads = cached_keys.shape[:2]
    group = heads // kv_heads
    rows = local_new * group
    tokens = n * local_new
    depth, cols = out_weight.shape
    chunks = n // (lanes // rows)
    all_keys = slots + new_pad
    block = tokens // ntp
    half = cols // col_tiles // 2
    vmem = pl.BlockSpec(memory_space=pltpu.VMEM)
    hbm = pl.BlockSpec(memory_space=pl.ANY)
    dma = pltpu.SemaphoreType.DMA
    flops = 4 * tokens * heads * slots * head_size + 2 * tokens * depth * cols
    out_shape = (
            jax.ShapeDtypeStruct((local_new, depth), bf16),
            jax.ShapeDtypeStruct((block, cols), bf16),
        )
    context, projected = pl.pallas_call(
        functools.partial(kernel, n, ntp, local_new, kv_heads, group, slots),
        out_shape=out_shape,
        in_specs=[hbm] * 8,
        out_specs=(vmem, vmem),
        scratch_shapes=[
            pltpu.VMEM((1, slots), jnp.int32),
            pltpu.VMEM((local_new * kv_heads, lanes), bf16),
            pltpu.VMEM((local_new * kv_heads, lanes), bf16),
            pltpu.SMEM((tokens,), jnp.int32),
            pltpu.VMEM((slots * kv_heads, lanes), bf16),
            pltpu.VMEM((slots * kv_heads, lanes), bf16),
            pltpu.VMEM((kv_heads, all_keys, lanes), bf16),
            pltpu.VMEM((kv_heads, all_keys, lanes), bf16),
            pltpu.VMEM((math.gcd(slots, 512) * kv_heads, lanes), f32),
            pltpu.VMEM((new_pad, lanes), f32),
            pltpu.VMEM((1, slots), f32),
            pltpu.VMEM((tokens * group, lanes), f32),
            pltpu.VMEM((tokens, heads, lanes), bf16),
            pltpu.VMEM((depth, cols), bf16),
            pltpu.VMEM((kv_heads, n, rows + stat_rows, lanes), bf16),
            pltpu.VMEM((kv_heads, n, rows + stat_rows, lanes), bf16),
            pltpu.VMEM((n * stat_rows, lanes), f32),
            pltpu.VMEM((lanes, n), f32),
            pltpu.VMEM((rows, lanes), f32),
            pltpu.VMEM((kv_heads, n, rows, lanes), bf16),
            pltpu.VMEM((tokens * group, lanes), f32),
            pltpu.VMEM((tokens, group * lanes), bf16),
            pltpu.VMEM((tokens, cols), f32),
            pltpu.VMEM((col_tiles, ntp, 2 * block, half), bf16),
            pltpu.VMEM((col_tiles, ntp, 2 * block, half), bf16),
            dma, dma, dma((5,)), dma((4 * kv_heads,)),
            dma, dma((kv_heads, chunks)), dma((kv_heads,)), dma((kv_heads,)),
            dma((kv_heads,)), dma((kv_heads,)), dma((col_tiles,)), dma((col_tiles,)),
        ],
        compiler_params=pltpu.CompilerParams(
            collective_id=0, has_side_effects=True, vmem_limit_bytes=56 * 2**20
        ),
        cost_estimate=pl.CostEstimate(
            flops=flops,
            bytes_accessed=2 * depth * cols + 4 * slots * kv_heads * head_size,
            transcendentals=tokens * heads * slots,
        ),
    )(
        queries,
        cached_keys.reshape(slots * kv_heads, head_size),
        cached_values.reshape(slots * kv_heads, head_size),
        cached_pos.reshape(1, slots),
        new_keys.reshape(local_new * kv_heads, head_size),
        new_values.reshape(local_new * kv_heads, head_size),
        new_pos,
        out_weight,
    )
    return pl.pallas_call(
        deliver,
        out_shape=out_shape,
        in_specs=[vmem, vmem],
        out_specs=(vmem, vmem),
    )(context, projected)


def solution(mesh):
    in_specs = (
        P("ctx", "tp", None),
        P("ctx", "tp", None),
        P("ctx", "tp", None),
        P("ctx"),
        P("ctx", "tp", None),
        P("ctx", "tp", None),
        P(),
        P("tp", "ctx"),
    )
    out_specs = (P("ctx", "tp"), P("tp", "ctx"))
    return jax.shard_map(
        functools.partial(per_device, mesh.shape["ctx"], mesh.shape["tp"]),
        mesh=mesh, in_specs=in_specs, out_specs=out_specs, check_vma=False,
    )
```

```python
import functools
import math

import jax
import jax.numpy as jnp
from jax import lax
from jax.experimental import pallas as pl
from jax.experimental.pallas import tpu as pltpu
from jax.sharding import PartitionSpec as P

masked_score = -1e30
MESH = pl.DeviceIdType.MESH
lanes = 128
new_pad = 128
col_tiles = 2
stat_rows = 16
bf16 = jnp.bfloat16
f32 = jnp.float32


def kernel(
    n, ntp, local_new, kv_heads, group, slots,
    q_hbm, k_hbm, v_hbm, pos_hbm, nk_hbm, nv_hbm, newpos_hbm, w_hbm,
    ctx_out, proj_out, pos_ref, nk_ref, nv_ref, newpos_ref,
    kraw, vraw, kh, vh, wide, small, bias_c, bias_n, qall, wbuf,
    onum, rnum, stat, wts, cown, call, cf, lhs, acc, dsend, drecv,
    k_sem, v_sem, i_sem, w_sem, q_send, q_recv, n_send, n_recv,
    c_send, c_recv, d_send, d_recv,
):
    me = lax.axis_index("ctx")
    tp = lax.axis_index("tp")
    rows = local_new * group
    per_chunk = lanes // rows
    chunks = n // per_chunk
    mine = me // per_chunk
    tokens = n * local_new
    depth = group * lanes
    coef = math.log2(math.e) / math.sqrt(lanes)

    k_copy = pltpu.make_async_copy(k_hbm, kraw, k_sem)
    v_copy = pltpu.make_async_copy(v_hbm, vraw, v_sem)
    small_copies = [
        pltpu.make_async_copy(src, dst, i_sem.at[i])
        for i, (src, dst) in enumerate(
            [(newpos_hbm, newpos_ref), (pos_hbm, pos_ref), (nk_hbm, nk_ref), (nv_hbm, nv_ref)]
        )
    ]
    own_q = pltpu.make_async_copy(
        q_hbm, qall.at[pl.ds(me * local_new, local_new)], i_sem.at[4]
    )
    for copy in small_copies:
        copy.start()
    own_q.start()
    k_copy.start()
    v_copy.start()
    w_parts = 4 * kv_heads
    w_rows = kv_heads * depth // w_parts
    w_copies = [
        pltpu.make_async_copy(
            w_hbm.at[pl.ds(i * w_rows, w_rows)], wbuf.at[pl.ds(i * w_rows, w_rows)], w_sem.at[i]
        )
        for i in range(w_parts)
    ]

    barrier = pltpu.get_barrier_semaphore()

    def greet(i, _):
        pl.semaphore_signal(
            barrier, inc=1, device_id={"ctx": lax.rem(me + i, n)}, device_id_type=MESH
        )
        return 0

    lax.fori_loop(1, n, greet, 0)
    for i in range(1, ntp):
        pl.semaphore_signal(
            barrier, inc=1, device_id={"tp": lax.rem(tp + i, ntp)}, device_id_type=MESH
        )
    for copy in small_copies:
        copy.wait()
    bias_c[...] = jnp.where(pos_ref[...] >= 0, 0.0, masked_score)
    lane = lax.broadcasted_iota(jnp.int32, (group, lanes), 1)
    key_pos = jnp.full((group, lanes), 2**30, jnp.int32)
    for j in range(local_new):
        key_pos = jnp.where(lane == j, newpos_ref[me * local_new + j], key_pos)

    def mask_new(t, _):
        bias_n[pl.ds(t * group, group), :] = jnp.where(
            key_pos <= newpos_ref[t], 0.0, masked_score
        )
        return 0

    lax.fori_loop(0, tokens, mask_new, 0)

    pl.semaphore_wait(barrier, n - 1 + ntp - 1)

    def q_copy(h, peer):
        heads = pl.ds(h * group, group)
        return pltpu.make_async_remote_copy(
            src_ref=q_hbm.at[:, heads],
            dst_ref=qall.at[pl.ds(me * local_new, local_new), heads],
            send_sem=q_send,
            recv_sem=q_recv.at[h, mine],
            device_id={"ctx": peer},
            device_id_type=MESH,
        )

    def num_copy(h, peer):
        return pltpu.make_async_remote_copy(
            src_ref=onum.at[h, peer],
            dst_ref=rnum.at[h, me],
            send_sem=n_send.at[h],
            recv_sem=n_recv.at[h],
            device_id={"ctx": peer},
            device_id_type=MESH,
        )

    def ctx_copy(h, peer):
        return pltpu.make_async_remote_copy(
            src_ref=call.at[h, me],
            dst_ref=call.at[h, me],
            send_sem=c_send.at[h],
            recv_sem=c_recv.at[h],
            device_id={"ctx": peer},
            device_id_type=MESH,
        )

    def part_copy(j, peer):
        return pltpu.make_async_remote_copy(
            src_ref=dsend.at[j, peer],
            dst_ref=drecv.at[j, tp],
            send_sem=d_send.at[j],
            recv_sem=d_recv.at[j],
            device_id={"tp": peer},
            device_id_type=MESH,
        )

    def await_bytes(ref, sem):
        pltpu.make_async_copy(ref, ref, sem).wait()

    def others(body):
        def step(i, _):
            body(lax.rem(me + i, n))
            return 0

        lax.fori_loop(1, n, step, 0)

    def chunk_at(i, sign):
        shift = lax.rem(i + chunks // 2 - 2, chunks - 1) + 1
        return lax.rem(mine + chunks + sign * shift, chunks)

    for h in range(kv_heads):
        for j in range(1, per_chunk):
            q_copy(h, mine * per_chunk + lax.rem(me + j, per_chunk)).start()

        def send_queries(i, _):
            c = chunk_at(i, 1)
            for j in range(per_chunk):
                q_copy(h, c * per_chunk + j).start()
            return 0

        lax.fori_loop(1, chunks, send_queries, 0)

    part = math.gcd(slots, 512)

    def split_heads(raw, new_ref, out):
        def step(i, _):
            wide[...] = raw[pl.ds(i * part * kv_heads, part * kv_heads), :].astype(f32)
            for h in range(kv_heads):
                out[h, pl.ds(i * part, part), :] = wide[
                    pl.ds(h, part, stride=kv_heads), :
                ].astype(bf16)
            return 0

        lax.fori_loop(0, slots // part, step, 0)
        wide[pl.ds(0, local_new * kv_heads), :] = new_ref[...].astype(f32)
        for h in range(kv_heads):
            small[...] = jnp.zeros_like(small)
            small[pl.ds(0, local_new), :] = wide[pl.ds(h, local_new, stride=kv_heads), :]
            out[h, pl.ds(slots, new_pad), :] = small[...].astype(bf16)

    k_copy.wait()
    v_copy.wait()
    for copy in w_copies:
        copy.start()
    split_heads(kraw, nk_ref, kh)
    split_heads(vraw, nv_ref, vh)
    own_q.wait()

    stat_row = lax.broadcasted_iota(jnp.int32, (stat_rows, lanes), 0)
    diag = lax.broadcasted_iota(jnp.int32, (lanes, lanes), 0) == lax.broadcasted_iota(
        jnp.int32, (lanes, lanes), 1
    )

    def attend(h, pair):
        heads = pl.ds(h * group, group)
        qs, news = [], []
        for c, others_of_chunk in pair:
            tok = c * per_chunk * local_new
            arrivals = len(others_of_chunk) * local_new
            if arrivals > 0:
                await_bytes(qall.at[pl.ds(0, arrivals), heads], q_recv.at[h, c])
        for c, _ in pair:
            tok = c * per_chunk * local_new
            qs.append(qall[pl.ds(tok, per_chunk * local_new), heads, :].reshape(lanes, lanes))
            news.append(bias_n[pl.ds(tok * group, lanes), :])
        s = lax.dot_general(
            jnp.concatenate(qs, axis=0), kh[h], (((1,), (1,)), ((), ())),
            preferred_element_type=f32,
        )
        old = s[:, :slots] + bias_c[...]
        new = s[:, slots:] + jnp.concatenate(news, axis=0)
        top = jnp.maximum(
            jnp.max(old, axis=1, keepdims=True), jnp.max(new, axis=1, keepdims=True)
        )
        old = jnp.exp2((old - top) * coef)
        new = jnp.exp2((new - top) * coef)
        total = jnp.sum(old, axis=1, keepdims=True) + jnp.sum(new, axis=1, keepdims=True)
        out = jnp.dot(old.astype(bf16), vh[h, :slots], preferred_element_type=f32)
        out += jnp.dot(new.astype(bf16), vh[h, slots:], preferred_element_type=f32)
        out = (out / total).astype(bf16)
        levels_all = top * coef + jnp.log2(total)
        for i, (c, others_of_chunk) in enumerate(pair):
            level = levels_all[i * lanes : (i + 1) * lanes]
            level = jnp.sum(jnp.where(diag, level, 0.0), axis=0, keepdims=True)
            levels = jnp.zeros((stat_rows, lanes), f32)
            for k in range(3):
                piece = level.astype(bf16).astype(f32)
                level = level - piece
                levels = jnp.where(stat_row == k, piece, levels)
            for j in range(per_chunk):
                at = i * lanes + j * rows
                onum[h, c * per_chunk + j, :rows] = out[at : at + rows]
                onum[h, c * per_chunk + j, rows:] = levels.astype(bf16)
        for c, others_of_chunk in reversed(pair):
            for peer in others_of_chunk:
                num_copy(h, peer).start()

    def whole_chunk(i):
        c = chunk_at(i, -1)
        return c, [c * per_chunk + j for j in range(per_chunk)]

    def attend_first(h):
        mates = [mine * per_chunk + lax.rem(me + j, per_chunk) for j in range(1, per_chunk)]
        attend(h, [(mine, mates), whole_chunk(1)])
        rnum[h, me] = onum[h, me]

    def attend_rest(h):
        def step(i, _):
            attend(h, [whole_chunk(2 * i), whole_chunk(2 * i + 1)])
            return 0

        lax.fori_loop(1, chunks // 2, step, 0)

    def combine(h):
        await_bytes(rnum.at[h, pl.ds(0, n - 1)], n_recv.at[h])
        stat[...] = rnum[h, :, rows:, :].reshape(n * stat_rows, lanes).astype(f32)
        level = stat[pl.ds(0, n, stride=stat_rows), :]
        for k in range(1, 3):
            level += stat[pl.ds(k, n, stride=stat_rows), :]
        factor = jnp.exp2(level - jnp.max(level, axis=0, keepdims=True))
        factor = factor / jnp.sum(factor, axis=0, keepdims=True)
        wts[...] = factor.T
        first = pl.multiple_of(lax.rem(me, per_chunk) * rows, rows)
        weight = wts[pl.ds(first, rows), :]
        context = jnp.zeros((rows, lanes), f32)
        for s in range(n):
            context += rnum[h, s, :rows].astype(f32) * weight[:, s : s + 1]
        call[h, me] = context.astype(bf16)
        others(lambda peer: ctx_copy(h, peer).start())
        cown[...] = context
        for g in range(group):
            at = (h * group + g) * lanes
            ctx_out[:, at : at + lanes] = cown[pl.ds(g, local_new, stride=group), :].astype(bf16)

    tile = proj_out.shape[1] // col_tiles
    half = tile // 2
    block = tokens // ntp

    def project(h):
        await_bytes(call.at[h, pl.ds(0, n - 1)], c_recv.at[h])
        cf[...] = call[h].reshape(tokens * group, lanes).astype(f32)
        for g in range(group):
            lhs[:, g * lanes : (g + 1) * lanes] = cf[pl.ds(g, tokens, stride=group), :].astype(bf16)
        for copy in w_copies[h * 4 : (h + 1) * 4]:
            copy.wait()
        for j in range(col_tiles):
            cols = slice(j * tile, (j + 1) * tile)
            term = jnp.dot(
                lhs[...], wbuf[h * depth : (h + 1) * depth, cols], preferred_element_type=f32
            )
            if h > 0:
                term += acc[:, cols]
            if h < kv_heads - 1:
                acc[:, cols] = term
                continue
            for r in range(ntp):
                slab = term[r * block : (r + 1) * block]
                slab = jnp.concatenate([slab[:, :half], slab[:, half:]], axis=0).astype(bf16)
                dsend[j, r] = slab

                @pl.when(tp != r)
                def _():
                    part_copy(j, r).start()

                @pl.when(tp == r)
                def _():
                    drecv[j, tp] = slab

    for h in range(kv_heads):
        attend_first(h)
        if h > 0:
            combine(h - 1)
        attend_rest(h)
    combine(kv_heads - 1)
    for h in range(kv_heads):
        project(h)

    for j in range(col_tiles):
        await_bytes(drecv.at[j, pl.ds(0, ntp - 1)], d_recv.at[j])
        total = drecv[j, 0].astype(f32)
        for r in range(1, ntp):
            total += drecv[j, r].astype(f32)
        proj_out[:, j * tile : (j + 1) * tile] = jnp.concatenate(
            [total[:block], total[block:]], axis=1
        ).astype(bf16)

    await_bytes(qall.at[pl.ds(0, (n - 1) * local_new)], q_send)
    for h in range(kv_heads):
        await_bytes(onum.at[h, pl.ds(0, n - 1)], n_send.at[h])
        await_bytes(call.at[h, pl.ds(0, n - 1)], c_send.at[h])
    for j in range(col_tiles):
        await_bytes(dsend.at[j, pl.ds(0, ntp - 1)], d_send.at[j])


def deliver(ctx_in, proj_in, ctx_out, proj_out):
    ctx_out[...] = ctx_in[...]
    proj_out[...] = proj_in[...]


def per_device(
    n, ntp, queries, cached_keys, cached_values, cached_pos, new_keys, new_values, new_pos,
    out_weight,
):
    local_new, heads, head_size = queries.shape
    slots, kv_heads = cached_keys.shape[:2]
    group = heads // kv_heads
    rows = local_new * group
    tokens = n * local_new
    depth, cols = out_weight.shape
    chunks = n // (lanes // rows)
    all_keys = slots + new_pad
    block = tokens // ntp
    half = cols // col_tiles // 2
    vmem = pl.BlockSpec(memory_space=pltpu.VMEM)
    hbm = pl.BlockSpec(memory_space=pl.ANY)
    dma = pltpu.SemaphoreType.DMA
    flops = 4 * tokens * heads * slots * head_size + 2 * tokens * depth * cols
    out_shape = (
            jax.ShapeDtypeStruct((local_new, depth), bf16),
            jax.ShapeDtypeStruct((block, cols), bf16),
        )
    context, projected = pl.pallas_call(
        functools.partial(kernel, n, ntp, local_new, kv_heads, group, slots),
        out_shape=out_shape,
        in_specs=[hbm] * 8,
        out_specs=(vmem, vmem),
        scratch_shapes=[
            pltpu.VMEM((1, slots), jnp.int32),
            pltpu.VMEM((local_new * kv_heads, lanes), bf16),
            pltpu.VMEM((local_new * kv_heads, lanes), bf16),
            pltpu.SMEM((tokens,), jnp.int32),
            pltpu.VMEM((slots * kv_heads, lanes), bf16),
            pltpu.VMEM((slots * kv_heads, lanes), bf16),
            pltpu.VMEM((kv_heads, all_keys, lanes), bf16),
            pltpu.VMEM((kv_heads, all_keys, lanes), bf16),
            pltpu.VMEM((math.gcd(slots, 512) * kv_heads, lanes), f32),
            pltpu.VMEM((new_pad, lanes), f32),
            pltpu.VMEM((1, slots), f32),
            pltpu.VMEM((tokens * group, lanes), f32),
            pltpu.VMEM((tokens, heads, lanes), bf16),
            pltpu.VMEM((depth, cols), bf16),
            pltpu.VMEM((kv_heads, n, rows + stat_rows, lanes), bf16),
            pltpu.VMEM((kv_heads, n, rows + stat_rows, lanes), bf16),
            pltpu.VMEM((n * stat_rows, lanes), f32),
            pltpu.VMEM((lanes, n), f32),
            pltpu.VMEM((rows, lanes), f32),
            pltpu.VMEM((kv_heads, n, rows, lanes), bf16),
            pltpu.VMEM((tokens * group, lanes), f32),
            pltpu.VMEM((tokens, group * lanes), bf16),
            pltpu.VMEM((tokens, cols), f32),
            pltpu.VMEM((col_tiles, ntp, 2 * block, half), bf16),
            pltpu.VMEM((col_tiles, ntp, 2 * block, half), bf16),
            dma, dma, dma((5,)), dma((4 * kv_heads,)),
            dma, dma((kv_heads, chunks)), dma((kv_heads,)), dma((kv_heads,)),
            dma((kv_heads,)), dma((kv_heads,)), dma((col_tiles,)), dma((col_tiles,)),
        ],
        compiler_params=pltpu.CompilerParams(
            collective_id=0, has_side_effects=True, vmem_limit_bytes=56 * 2**20
        ),
        cost_estimate=pl.CostEstimate(
            flops=flops,
            bytes_accessed=2 * depth * cols + 4 * slots * kv_heads * head_size,
            transcendentals=tokens * heads * slots,
        ),
    )(
        queries,
        cached_keys.reshape(slots * kv_heads, head_size),
        cached_values.reshape(slots * kv_heads, head_size),
        cached_pos.reshape(1, slots),
        new_keys.reshape(local_new * kv_heads, head_size),
        new_values.reshape(local_new * kv_heads, head_size),
        new_pos,
        out_weight,
    )
    return pl.pallas_call(
        deliver,
        out_shape=out_shape,
        in_specs=[vmem, vmem],
        out_specs=(vmem, vmem),
    )(context, projected)


def solution(mesh):
    in_specs = (
        P("ctx", "tp", None),
        P("ctx", "tp", None),
        P("ctx", "tp", None),
        P("ctx"),
        P("ctx", "tp", None),
        P("ctx", "tp", None),
        P(),
        P("tp", "ctx"),
    )
    out_specs = (P("ctx", "tp"), P("tp", "ctx"))
    return jax.shard_map(
        functools.partial(per_device, mesh.shape["ctx"], mesh.shape["tp"]),
        mesh=mesh, in_specs=in_specs, out_specs=out_specs, check_vma=False,
    )
```

```python
import functools
import math

import jax
import jax.numpy as jnp
from jax import lax
from jax.experimental import pallas as pl
from jax.experimental.pallas import tpu as pltpu
from jax.sharding import PartitionSpec as P

masked_score = -1e30
MESH = pl.DeviceIdType.MESH
lanes = 128
new_pad = 128
col_tiles = 2
stat_rows = 16
bf16 = jnp.bfloat16
f32 = jnp.float32


def kernel(
    n, ntp, local_new, kv_heads, group, slots,
    q_hbm, k_hbm, v_hbm, pos_hbm, nk_hbm, nv_hbm, newpos_hbm, w_hbm,
    ctx_out, proj_out, pos_ref, nk_ref, nv_ref, newpos_ref,
    kraw, vraw, kh, vh, wide, small, bias_c, bias_n, qall, wbuf,
    onum, rnum, stat, wts, cown, call, cf, lhs, acc, dsend, drecv,
    k_sem, v_sem, i_sem, w_sem, q_send, q_recv, n_send, n_recv,
    c_send, c_recv, d_send, d_recv,
):
    me = lax.axis_index("ctx")
    tp = lax.axis_index("tp")
    rows = local_new * group
    per_chunk = lanes // rows
    chunks = n // per_chunk
    mine = me // per_chunk
    num_rows = kv_heads * rows
    tokens = n * local_new
    depth = group * lanes
    coef = math.log2(math.e) / math.sqrt(lanes)

    k_copy = pltpu.make_async_copy(k_hbm, kraw, k_sem)
    v_copy = pltpu.make_async_copy(v_hbm, vraw, v_sem)
    small_copies = [
        pltpu.make_async_copy(src, dst, i_sem.at[i])
        for i, (src, dst) in enumerate(
            [(newpos_hbm, newpos_ref), (pos_hbm, pos_ref), (nk_hbm, nk_ref), (nv_hbm, nv_ref)]
        )
    ]
    own_q = pltpu.make_async_copy(
        q_hbm, qall.at[pl.ds(me * local_new, local_new)], i_sem.at[4]
    )
    for copy in small_copies:
        copy.start()
    own_q.start()
    k_copy.start()
    v_copy.start()
    w_parts = 4 * kv_heads
    w_rows = kv_heads * depth // w_parts
    w_copies = [
        pltpu.make_async_copy(
            w_hbm.at[pl.ds(i * w_rows, w_rows)], wbuf.at[pl.ds(i * w_rows, w_rows)], w_sem.at[i]
        )
        for i in range(w_parts)
    ]

    barrier = pltpu.get_barrier_semaphore()

    def greet(i, _):
        pl.semaphore_signal(
            barrier, inc=1, device_id={"ctx": lax.rem(me + i, n)}, device_id_type=MESH
        )
        return 0

    lax.fori_loop(1, n, greet, 0)
    for i in range(1, ntp):
        pl.semaphore_signal(
            barrier, inc=1, device_id={"tp": lax.rem(tp + i, ntp)}, device_id_type=MESH
        )
    pl.semaphore_wait(barrier, n - 1 + ntp - 1)

    def q_copy(peer):
        return pltpu.make_async_remote_copy(
            src_ref=q_hbm,
            dst_ref=qall.at[pl.ds(me * local_new, local_new)],
            send_sem=q_send,
            recv_sem=q_recv.at[mine],
            device_id={"ctx": peer},
            device_id_type=MESH,
        )

    def num_copy(peer):
        return pltpu.make_async_remote_copy(
            src_ref=onum.at[peer],
            dst_ref=rnum.at[me],
            send_sem=n_send,
            recv_sem=n_recv,
            device_id={"ctx": peer},
            device_id_type=MESH,
        )

    def ctx_copy(h, peer):
        return pltpu.make_async_remote_copy(
            src_ref=call.at[h, me],
            dst_ref=call.at[h, me],
            send_sem=c_send.at[h],
            recv_sem=c_recv.at[h],
            device_id={"ctx": peer},
            device_id_type=MESH,
        )

    def part_copy(j, peer):
        return pltpu.make_async_remote_copy(
            src_ref=dsend.at[j, peer],
            dst_ref=drecv.at[j, tp],
            send_sem=d_send.at[j],
            recv_sem=d_recv.at[j],
            device_id={"tp": peer},
            device_id_type=MESH,
        )

    def await_bytes(ref, sem):
        pltpu.make_async_copy(ref, ref, sem).wait()

    def others(body):
        def step(i, _):
            body(lax.rem(me + i, n))
            return 0

        lax.fori_loop(1, n, step, 0)

    def chunk_at(i, sign):
        shift = lax.rem(i + chunks // 2 - 2, chunks - 1) + 1
        return lax.rem(mine + chunks + sign * shift, chunks)

    for j in range(1, per_chunk):
        q_copy(mine * per_chunk + lax.rem(me + j, per_chunk)).start()

    def send_queries(i, _):
        c = chunk_at(i, 1)
        for j in range(per_chunk):
            q_copy(c * per_chunk + j).start()
        return 0

    lax.fori_loop(1, chunks, send_queries, 0)

    for copy in small_copies:
        copy.wait()
    bias_c[...] = jnp.where(pos_ref[...] >= 0, 0.0, masked_score)
    lane = lax.broadcasted_iota(jnp.int32, (group, lanes), 1)
    key_pos = jnp.full((group, lanes), 2**30, jnp.int32)
    for j in range(local_new):
        key_pos = jnp.where(lane == j, newpos_ref[me * local_new + j], key_pos)

    def mask_new(t, _):
        bias_n[pl.ds(t * group, group), :] = jnp.where(
            key_pos <= newpos_ref[t], 0.0, masked_score
        )
        return 0

    lax.fori_loop(0, tokens, mask_new, 0)

    part = math.gcd(slots, 512)

    def split_heads(raw, new_ref, out):
        def step(i, _):
            wide[...] = raw[pl.ds(i * part * kv_heads, part * kv_heads), :].astype(f32)
            for h in range(kv_heads):
                out[h, pl.ds(i * part, part), :] = wide[
                    pl.ds(h, part, stride=kv_heads), :
                ].astype(bf16)
            return 0

        lax.fori_loop(0, slots // part, step, 0)
        wide[pl.ds(0, local_new * kv_heads), :] = new_ref[...].astype(f32)
        for h in range(kv_heads):
            small[...] = jnp.zeros_like(small)
            small[pl.ds(0, local_new), :] = wide[pl.ds(h, local_new, stride=kv_heads), :]
            out[h, pl.ds(slots, new_pad), :] = small[...].astype(bf16)

    k_copy.wait()
    v_copy.wait()
    for copy in w_copies:
        copy.start()
    split_heads(kraw, nk_ref, kh)
    split_heads(vraw, nv_ref, vh)
    own_q.wait()

    stat_row = lax.broadcasted_iota(jnp.int32, (stat_rows, lanes), 0)
    diag = lax.broadcasted_iota(jnp.int32, (lanes, lanes), 0) == lax.broadcasted_iota(
        jnp.int32, (lanes, lanes), 1
    )

    def attend(c, others_of_chunk):
        tok = c * per_chunk * local_new
        arrivals = len(others_of_chunk) * local_new
        if arrivals > 0:
            await_bytes(qall.at[pl.ds(0, arrivals)], q_recv.at[c])
        scores = []
        for h in range(kv_heads):
            q = qall[pl.ds(tok, per_chunk * local_new), pl.ds(h * group, group), :]
            scores.append(
                lax.dot_general(
                    q.reshape(lanes, lanes), kh[h], (((1,), (1,)), ((), ())),
                    preferred_element_type=f32,
                )
            )
        levels = jnp.zeros((stat_rows, lanes), f32)
        for h in range(kv_heads):
            s = scores[h]
            old = s[:, :slots] + bias_c[...]
            new = s[:, slots:] + bias_n[pl.ds(tok * group, lanes), :]
            top = jnp.maximum(
                jnp.max(old, axis=1, keepdims=True), jnp.max(new, axis=1, keepdims=True)
            )
            old = jnp.exp2((old - top) * coef)
            new = jnp.exp2((new - top) * coef)
            total = jnp.sum(old, axis=1, keepdims=True) + jnp.sum(new, axis=1, keepdims=True)
            out = jnp.dot(old.astype(bf16), vh[h, :slots], preferred_element_type=f32)
            out += jnp.dot(new.astype(bf16), vh[h, slots:], preferred_element_type=f32)
            out = (out / total).astype(bf16)
            level = top * coef + jnp.log2(total)
            level = jnp.sum(jnp.where(diag, level, 0.0), axis=0, keepdims=True)
            for k in range(3):
                piece = level.astype(bf16).astype(f32)
                level = level - piece
                levels = jnp.where(stat_row == 3 * h + k, piece, levels)
            for j in range(per_chunk):
                onum[c * per_chunk + j, h * rows : (h + 1) * rows] = out[
                    j * rows : (j + 1) * rows
                ]
        for j in range(per_chunk):
            onum[c * per_chunk + j, num_rows:] = levels.astype(bf16)
        for peer in others_of_chunk:
            num_copy(peer).start()

    def attend_all():
        attend(
            mine,
            [
                mine * per_chunk + lax.rem(me + j, per_chunk) for j in range(1, per_chunk)
            ],
        )
        rnum[me] = onum[me]

        def step(i, _):
            c = chunk_at(i, -1)
            attend(c, [c * per_chunk + j for j in range(per_chunk)])
            return 0

        lax.fori_loop(1, chunks, step, 0)

    def combine(h):
        level = stat[pl.ds(3 * h, n, stride=stat_rows), :]
        for k in range(1, 3):
            level += stat[pl.ds(3 * h + k, n, stride=stat_rows), :]
        factor = jnp.exp2(level - jnp.max(level, axis=0, keepdims=True))
        factor = factor / jnp.sum(factor, axis=0, keepdims=True)
        wts[...] = factor.T
        first = pl.multiple_of(lax.rem(me, per_chunk) * rows, rows)
        weight = wts[pl.ds(first, rows), :]
        context = jnp.zeros((rows, lanes), f32)
        for s in range(n):
            context += rnum[s, h * rows : (h + 1) * rows].astype(f32) * weight[:, s : s + 1]
        call[h, me] = context.astype(bf16)
        others(lambda peer: ctx_copy(h, peer).start())
        cown[...] = context
        for g in range(group):
            at = (h * group + g) * lanes
            ctx_out[:, at : at + lanes] = cown[pl.ds(g, local_new, stride=group), :].astype(bf16)

    tile = proj_out.shape[1] // col_tiles
    half = tile // 2
    block = tokens // ntp

    def project(h):
        await_bytes(call.at[h, pl.ds(0, n - 1)], c_recv.at[h])
        cf[...] = call[h].reshape(tokens * group, lanes).astype(f32)
        for g in range(group):
            lhs[:, g * lanes : (g + 1) * lanes] = cf[pl.ds(g, tokens, stride=group), :].astype(bf16)
        for copy in w_copies[h * 4 : (h + 1) * 4]:
            copy.wait()
        for j in range(col_tiles):
            cols = slice(j * tile, (j + 1) * tile)
            term = jnp.dot(
                lhs[...], wbuf[h * depth : (h + 1) * depth, cols], preferred_element_type=f32
            )
            if h > 0:
                term += acc[:, cols]
            if h < kv_heads - 1:
                acc[:, cols] = term
                continue
            for r in range(ntp):
                slab = term[r * block : (r + 1) * block]
                slab = jnp.concatenate([slab[:, :half], slab[:, half:]], axis=0).astype(bf16)
                dsend[j, r] = slab

                @pl.when(tp != r)
                def _():
                    part_copy(j, r).start()

                @pl.when(tp == r)
                def _():
                    drecv[j, tp] = slab

    attend_all()
    await_bytes(rnum.at[pl.ds(0, n - 1)], n_recv)
    stat[...] = rnum[:, num_rows:, :].reshape(n * stat_rows, lanes).astype(f32)
    for h in range(kv_heads):
        combine(h)
    for h in range(kv_heads):
        project(h)

    for j in range(col_tiles):
        await_bytes(drecv.at[j, pl.ds(0, ntp - 1)], d_recv.at[j])
        total = drecv[j, 0].astype(f32)
        for r in range(1, ntp):
            total += drecv[j, r].astype(f32)
        proj_out[:, j * tile : (j + 1) * tile] = jnp.concatenate(
            [total[:block], total[block:]], axis=1
        ).astype(bf16)

    await_bytes(qall.at[pl.ds(0, (n - 1) * local_new)], q_send)
    await_bytes(onum.at[pl.ds(0, n - 1)], n_send)
    for h in range(kv_heads):
        await_bytes(call.at[h, pl.ds(0, n - 1)], c_send.at[h])
    for j in range(col_tiles):
        await_bytes(dsend.at[j, pl.ds(0, ntp - 1)], d_send.at[j])


def deliver(ctx_in, proj_in, ctx_out, proj_out):
    ctx_out[...] = ctx_in[...]
    proj_out[...] = proj_in[...]


def per_device(
    n, ntp, queries, cached_keys, cached_values, cached_pos, new_keys, new_values, new_pos,
    out_weight,
):
    local_new, heads, head_size = queries.shape
    slots, kv_heads = cached_keys.shape[:2]
    group = heads // kv_heads
    rows = local_new * group
    tokens = n * local_new
    depth, cols = out_weight.shape
    chunks = n // (lanes // rows)
    all_keys = slots + new_pad
    block = tokens // ntp
    half = cols // col_tiles // 2
    vmem = pl.BlockSpec(memory_space=pltpu.VMEM)
    hbm = pl.BlockSpec(memory_space=pl.ANY)
    dma = pltpu.SemaphoreType.DMA
    flops = 4 * tokens * heads * slots * head_size + 2 * tokens * depth * cols
    out_shape = (
            jax.ShapeDtypeStruct((local_new, depth), bf16),
            jax.ShapeDtypeStruct((block, cols), bf16),
        )
    context, projected = pl.pallas_call(
        functools.partial(kernel, n, ntp, local_new, kv_heads, group, slots),
        out_shape=out_shape,
        in_specs=[hbm] * 8,
        out_specs=(vmem, vmem),
        scratch_shapes=[
            pltpu.VMEM((1, slots), jnp.int32),
            pltpu.VMEM((local_new * kv_heads, lanes), bf16),
            pltpu.VMEM((local_new * kv_heads, lanes), bf16),
            pltpu.SMEM((tokens,), jnp.int32),
            pltpu.VMEM((slots * kv_heads, lanes), bf16),
            pltpu.VMEM((slots * kv_heads, lanes), bf16),
            pltpu.VMEM((kv_heads, all_keys, lanes), bf16),
            pltpu.VMEM((kv_heads, all_keys, lanes), bf16),
            pltpu.VMEM((math.gcd(slots, 512) * kv_heads, lanes), f32),
            pltpu.VMEM((new_pad, lanes), f32),
            pltpu.VMEM((1, slots), f32),
            pltpu.VMEM((tokens * group, lanes), f32),
            pltpu.VMEM((tokens, heads, lanes), bf16),
            pltpu.VMEM((depth, cols), bf16),
            pltpu.VMEM((n, kv_heads * rows + stat_rows, lanes), bf16),
            pltpu.VMEM((n, kv_heads * rows + stat_rows, lanes), bf16),
            pltpu.VMEM((n * stat_rows, lanes), f32),
            pltpu.VMEM((lanes, n), f32),
            pltpu.VMEM((rows, lanes), f32),
            pltpu.VMEM((kv_heads, n, rows, lanes), bf16),
            pltpu.VMEM((tokens * group, lanes), f32),
            pltpu.VMEM((tokens, group * lanes), bf16),
            pltpu.VMEM((tokens, cols), f32),
            pltpu.VMEM((col_tiles, ntp, 2 * block, half), bf16),
            pltpu.VMEM((col_tiles, ntp, 2 * block, half), bf16),
            dma, dma, dma((5,)), dma((4 * kv_heads,)),
            dma, dma((chunks,)), dma, dma,
            dma((kv_heads,)), dma((kv_heads,)), dma((col_tiles,)), dma((col_tiles,)),
        ],
        compiler_params=pltpu.CompilerParams(
            collective_id=0, has_side_effects=True, vmem_limit_bytes=56 * 2**20
        ),
        cost_estimate=pl.CostEstimate(
            flops=flops,
            bytes_accessed=2 * depth * cols + 4 * slots * kv_heads * head_size,
            transcendentals=tokens * heads * slots,
        ),
    )(
        queries,
        cached_keys.reshape(slots * kv_heads, head_size),
        cached_values.reshape(slots * kv_heads, head_size),
        cached_pos.reshape(1, slots),
        new_keys.reshape(local_new * kv_heads, head_size),
        new_values.reshape(local_new * kv_heads, head_size),
        new_pos,
        out_weight,
    )
    return pl.pallas_call(
        deliver,
        out_shape=out_shape,
        in_specs=[vmem, vmem],
        out_specs=(vmem, vmem),
    )(context, projected)


def solution(mesh):
    in_specs = (
        P("ctx", "tp", None),
        P("ctx", "tp", None),
        P("ctx", "tp", None),
        P("ctx"),
        P("ctx", "tp", None),
        P("ctx", "tp", None),
        P(),
        P("tp", "ctx"),
    )
    out_specs = (P("ctx", "tp"), P("tp", "ctx"))
    return jax.shard_map(
        functools.partial(per_device, mesh.shape["ctx"], mesh.shape["tp"]),
        mesh=mesh, in_specs=in_specs, out_specs=out_specs, check_vma=False,
    )
```
